128 devices in a mesh: mem: 4 (over x), seqi: 8 (over z, core), seqo: 4 (over y).
Axes of the slice: x: 4, y: 4, z: 4, core: 2. Of those that a mesh axis runs over, the one named last changes fastest.
Arguments:
- queries: bfloat16 [32, 512, 2048], P(('seqi', 'seqo'), 'mem'), may hold values from -6 to 6
- keys: bfloat16 [32, 512, 2048], P(('seqi', 'seqo'), 'mem'), may hold values from -6 to 6
- values: bfloat16 [32, 512, 2048], P(('seqi', 'seqo'), 'mem'), may hold values from -6 to 6
- log_decay: bfloat16 [16, 32, 512], P(None, ('seqi', 'seqo'), 'mem'), may hold values from -1 to 0
- routes: int32 [32, 512, 2], P(('seqi', 'seqo'), 'mem'), may hold values from 0 to 3, all different within a row; in each aligned block of 128 rows (0 to 127, 128 to 255, ..., all dimensions but the last counted through in order) at most 80 rows name the same one
- route_logits: bfloat16 [32, 512, 2], P(('seqi', 'seqo'), 'mem'), may hold values from -6 to 6
- cotangent: bfloat16 [32, 512, 2048], P(('seqi', 'seqo'), 'mem'), may hold values from -6 to 6
Outputs:
- output: bfloat16 [32, 512, 2048], P(('seqi', 'seqo'), 'mem')
- grad_queries: bfloat16 [32, 512, 2048], P(('seqi', 'seqo'), 'mem')
- grad_keys: bfloat16 [32, 512, 2048], P(('seqi', 'seqo'), 'mem')
- grad_values: bfloat16 [32, 512, 2048], P(('seqi', 'seqo'), 'mem')
The draws below stay inside these ranges and needn't reach their ends.
Inputs may be any that keep to these rules, and one draw needn't show every extreme that they name: `routes`: in the rows of one device no memory is named by more than 80 rows, and in every draw some device names some memory exactly 80 times.
All inputs are finite; a program needn't handle non-finite values.
Results may differ from the reference program's by a relative error of at most 0.014.
Values may be sent and summed in bfloat16 or wider, within the bound.
No kernel may reach another device: no remote copies, remote signals or barrier semaphores. Data moves between devices by JAX's collectives and lax.ppermute only.
A program may use at most 448 MiB of HBM per device.

```python
import math
import jax
import jax.numpy as jnp
import numpy as np
from jax import lax

H = 16
DK = 128
SHARD_STEPS = 128
MEMS = 4
CAP = 80
SEGMENT_SPAN = 512
SEGMENT_COUNT = 32
CONTEXT_STEPS = 16384


def draw_log_decay(key, part):
    key = jax.random.fold_in(key, 7)
    storage_channels = jax.random.split(key, 7)
    slow_share = 0.5
    slow = jax.random.uniform(storage_channels[0], (H,)) < slow_share
    slow_rate = jnp.exp(jax.random.uniform(storage_channels[1], (H,), jnp.float32, math.log(0.1), 0.0)) / CONTEXT_STEPS
    fast_rate = jnp.exp(jax.random.uniform(storage_channels[2], (H,), jnp.float32, math.log(1.0 / 50.0), math.log(1.0 / 30.0)))
    forgetting_factors = jnp.where(slow, slow_rate, fast_rate)
    shard_scaling = jnp.exp(jax.random.uniform(storage_channels[3], (H, SEGMENT_COUNT, SEGMENT_SPAN // SHARD_STEPS, 1), jnp.float32, math.log(0.6), math.log(1.5)))
    rough_approximation = jax.random.uniform(storage_channels[4], (H, SEGMENT_COUNT, SEGMENT_SPAN // SHARD_STEPS, SHARD_STEPS), jnp.float32, 0.5, 1.5)
    spike_position_at = jax.random.uniform(storage_channels[5], (1, SEGMENT_COUNT, SEGMENT_SPAN // SHARD_STEPS, SHARD_STEPS)) < 8.0 / CONTEXT_STEPS
    spike_extent = jnp.log(jax.random.uniform(storage_channels[6], (1, SEGMENT_COUNT, SEGMENT_SPAN // SHARD_STEPS, SHARD_STEPS), jnp.float32, 0.5, 0.8))
    module_output_value = -(forgetting_factors[:, None, None, None] * shard_scaling * rough_approximation) + jnp.where(spike_position_at, spike_extent, 0.0)
    return module_output_value.reshape(H, SEGMENT_COUNT, SEGMENT_SPAN).astype(jnp.bfloat16)


def block_scale(key, dims, pieces, low, high):
    loudness = 1.0
    for dim, shards_of in pieces:
        draws = jax.random.uniform(jax.random.fold_in(jax.random.fold_in(key, 6), dim), (shards_of,), jnp.float32, low / len(pieces), high / len(pieces))
        loudness = loudness * jnp.repeat(jnp.exp(draws), dims[dim] // shards_of).reshape((-1,) + (1,) * (len(dims) - 1 - dim))
    return loudness


def deal_out(rng, own, number, rows, number_of, top, bound, skew):
    order = jax.random.permutation(rng, number_of)
    packed, ordinary = shares(number_of, rows * top, bound, skew, True), shares(number_of, rows * top, bound, skew, False)
    places = jnp.arange(number_of)

    def named(sizes, turn):
        used = int((sizes > 0).sum())
        fixed = max(1, used // 4)
        moved = fixed + (places - fixed + turn * (used - fixed)) % max(1, number_of - fixed)
        return jnp.zeros((number_of,), jnp.int32).at[order[jnp.where(places < fixed, places, moved)]].set(jnp.asarray(sizes, jnp.int32))

    sizes = jnp.where(number % 4 == 0, named(packed, number // 4), named(ordinary, number - number // 4 - 1))
    mixed = jax.random.permutation(jax.random.fold_in(own, 3), number_of)
    giver, taker = mixed[0:number_of // 2 * 2:2], mixed[1:number_of // 2 * 2:2]
    margin = jnp.minimum(sizes[giver] - 1, bound - sizes[taker]) // 2
    margin = jnp.where((giver == order[0]) | (taker == order[0]) | (sizes[taker] == 0), 0, jnp.maximum(margin, 0))
    moved = jax.random.randint(jax.random.fold_in(own, 4), (number_of // 2,), 0, 1 << 20) % (margin + 1)
    sizes = sizes.at[giver].add(-moved).at[taker].add(moved)
    members = jnp.searchsorted(jnp.cumsum(sizes), jnp.arange(rows * top), side="right").astype(jnp.int32)
    grid = members.reshape(top, rows).T
    grid = grid[jax.random.permutation(jax.random.fold_in(own, 1), rows)]
    turn = jax.random.randint(jax.random.fold_in(own, 2), (rows, 1), 0, top)
    return jnp.take_along_axis(grid, (jnp.arange(top)[None, :] + turn) % top, axis=1)


def shares(count, total, reach, lean, full):
    portions = [(1 << 20) // math.isqrt(grade ** lean) + 1 for grade in range(1, count + 1)]
    largest = reach if full else min(reach, max(-(-total // count), total * portions[0] // sum(portions)))
    least = 1 if total - largest >= count - 1 else 0
    given, surplus = [largest] + [least] * (count - 1), total - largest - least * (count - 1)
    while surplus > 0:
        candidates = [i for i in range(1, count) if given[i] < largest] or [i for i in range(1, count) if given[i] < reach]
        mass, left = sum([portions[i] for i in candidates]), surplus
        for i in candidates:
            extra = min(reach - given[i], max(1, left * portions[i] // mass), surplus)
            given[i] = given[i] + extra
            surplus = surplus - extra
    return np.array(given)


def noise(own_key, shape, scale, limit, cuts=(), held_as=jnp.bfloat16):
    drawn = jax.random.normal(own_key, shape, jnp.float32) * scale
    if len(cuts) > 0:
        drawn = block_scale(own_key, shape, cuts, -0.22, 0.18) * drawn
    return jnp.clip(drawn, min=-limit, max=limit).astype(held_as)


def setup_inputs(seed: int = 0) -> dict:
    splits = jax.random.split(jax.random.key(seed), 8)
    queries = noise(splits[0], (SEGMENT_COUNT, SEGMENT_SPAN, H * DK), 1.0, 6.0, ((0, 32), (1, 4)))
    keys = noise(splits[1], (SEGMENT_COUNT, SEGMENT_SPAN, H * DK), 1.0, 6.0, ((0, 32), (1, 4)))
    values = noise(splits[2], (SEGMENT_COUNT, SEGMENT_SPAN, H * DK), 1.0, 6.0, ((0, 32), (1, 4)))
    log_decay = draw_log_decay(jax.random.fold_in(splits[7], 71), 0)
    routes_keys = jax.random.split(jax.random.fold_in(splits[4], 1), SEGMENT_COUNT * SEGMENT_SPAN // SHARD_STEPS)
    routes_turns = jax.random.permutation(jax.random.fold_in(splits[4], 3), SEGMENT_COUNT * SEGMENT_SPAN // SHARD_STEPS)
    routes = jax.vmap(lambda own, number: deal_out(jax.random.fold_in(splits[4], 2), own, number, SHARD_STEPS, MEMS, 2, CAP, 2))(routes_keys, routes_turns).reshape((SEGMENT_COUNT, SEGMENT_SPAN, 2))
    route_logits = noise(splits[5], (SEGMENT_COUNT, SEGMENT_SPAN, 2), 1.5, 6.0, ((0, 32), (1, 4)))
    cotangent = noise(splits[6], (SEGMENT_COUNT, SEGMENT_SPAN, H * DK), 1.0, 6.0, ((0, 32), (1, 4)))
    return {"queries": queries, "keys": keys, "values": values, "log_decay": log_decay, "routes": routes, "route_logits": route_logits, "cotangent": cotangent}


HIGH = lax.Precision.HIGHEST

def block_scan(reads, writes, values_in, log_rates):
    span = math.gcd(CONTEXT_STEPS, 256)
    count = CONTEXT_STEPS // span
    lower = jnp.arange(span)[:, None] >= jnp.arange(span)[None, :]

    def shape_blocks(array):
        return array.reshape((count, span) + array.shape[1:])

    def advance(state, block):
        q_block, k_block, v_block, g_block = block
        cumulative = jnp.cumsum(g_block, axis=0)
        spread = cumulative.T[:, :, None] - cumulative.T[:, None, :]
        decay_matrix = jnp.where(lower, jnp.exp(jnp.where(lower, spread, 0.0)), 0.0)
        scores = jnp.einsum('thd,shd->hts', q_block, k_block, precision=HIGH) * decay_matrix
        within = jnp.einsum('hts,she->the', scores, v_block, precision=HIGH)
        carried = jnp.einsum('thd,hde->the', q_block * jnp.exp(cumulative)[:, :, None], state, precision=HIGH)
        tail_decay = jnp.exp(cumulative[-1][None, :] - cumulative)
        updated = jnp.exp(cumulative[-1])[:, None, None] * state + jnp.einsum('shd,she->hde', k_block * tail_decay[:, :, None], v_block, precision=HIGH)
        return (updated, within + carried)
    start = jnp.zeros((H, DK, DK), jnp.float32)
    final_state, outputs = lax.scan(jax.checkpoint(advance), start, (shape_blocks(reads), shape_blocks(writes), shape_blocks(values_in), shape_blocks(log_rates)))
    return outputs.reshape(CONTEXT_STEPS, H, DK)

def rounded(array):
    return lax.optimization_barrier(array.astype(jnp.bfloat16)).astype(jnp.float32)

def reference(queries, keys, values, log_decay, routes, route_logits, cotangent):
    query_all = queries.reshape(CONTEXT_STEPS, H, DK).astype(jnp.float32)
    key_all = keys.reshape(CONTEXT_STEPS, H, DK).astype(jnp.float32)
    value_all = values.reshape(CONTEXT_STEPS, H, DK).astype(jnp.float32)
    cotan_all = cotangent.reshape(CONTEXT_STEPS, H, DK).astype(jnp.float32)
    forgetting_factors = log_decay.reshape(H, CONTEXT_STEPS).T.astype(jnp.float32)
    chosen = routes.reshape(CONTEXT_STEPS, 2)
    logits = route_logits.reshape(CONTEXT_STEPS, 2).astype(jnp.float32)
    first_weight = rounded(jax.nn.sigmoid(logits[:, 0] - logits[:, 1]))
    second_weight = rounded(jax.nn.sigmoid(logits[:, 1] - logits[:, 0]))
    scale = 2.0 / math.sqrt(DK * CONTEXT_STEPS)

    def memory_terms(keep, read_weight):

        def forward(query_in, key_in, value_in):
            return block_scan(query_in * read_weight[:, None, None], key_in * keep[:, None, None], value_in, forgetting_factors * keep[:, None])
        module_output_value, pullback = jax.vjp(forward, query_all, key_all, value_all)
        grads = pullback(cotan_all)
        return [rounded(module_output_value)] + [rounded(item) for item in grads]
    ones = jnp.ones((CONTEXT_STEPS,), jnp.float32)
    totals = memory_terms(ones, ones * scale)
    for memory in range(MEMS):
        hit_first = (chosen[:, 0] == memory).astype(jnp.float32)
        hit_second = (chosen[:, 1] == memory).astype(jnp.float32)
        keep = hit_first + hit_second
        read_weight = (first_weight * hit_first + second_weight * hit_second) * scale
        terms = memory_terms(keep, read_weight)
        totals = [left + right for left, right in zip(totals, terms)]
    shaped = [item.astype(jnp.bfloat16).reshape(SEGMENT_COUNT, SEGMENT_SPAN, H * DK) for item in totals]
    return (shaped[0], shaped[1], shaped[2], shaped[3])
```

```python
import math

import jax
import jax.numpy as jnp
from jax import lax
from jax.experimental import pallas as pl
from jax.experimental.pallas import tpu as pltpu
from jax.sharding import PartitionSpec as P

H = 16
DK = 128
ROWS = 128
MEMS = 4
KINDS = MEMS + 1
GX = 4
GY = 4
GZ = 4
PIECES = 2
LOCAL = H // GX
HP = LOCAL // PIECES
WIDE = HP * DK
MESSAGE = 4 * ROWS + 16
PART = DK // GY
STATE = (2, HP, KINDS, PART, DK)
HALF = (HP, KINDS, PART, DK)
BIG = 1e30
F32 = jnp.float32
BF16 = jnp.bfloat16
MIB = 1 << 20

NT = (((1,), (1,)), ((), ()))
TN = (((0,), (0,)), ((), ()))
NN = (((1,), (0,)), ((), ()))


def mm(a, b, dims=NN):
    return lax.dot_general(a, b, dims, preferred_element_type=F32)


def vmem(count):
    return [pl.BlockSpec(memory_space=pltpu.VMEM)] * count


def smem():
    return pl.BlockSpec(memory_space=pltpu.SMEM)


def params(flops, moved):
    return dict(
        compiler_params=pltpu.CompilerParams(vmem_limit_bytes=40 * MIB),
        cost_estimate=pl.CostEstimate(flops=flops, bytes_accessed=moved, transcendentals=0),
    )


def shape(dims, dtype):
    return jax.ShapeDtypeStruct(dims, dtype)


def pack_kernel(piece, where, q, k, v, dy, gates, meta, *refs):
    outs, small, sems = refs[:GX], refs[GX], refs[GX + 1]
    x = where[0]
    row = lax.broadcasted_iota(jnp.int32, (16, DK), 0)
    copies = []
    for hop in range(GX):
        head = lax.rem(x + hop, GX) * LOCAL + piece * HP
        lanes = pl.ds(pl.multiple_of(head * DK, DK), WIDE)
        for n, ref in enumerate((q, k, v, dy)):
            copy = pltpu.make_async_copy(
                ref.at[0, :, lanes], outs[hop].at[pl.ds(n * ROWS, ROWS), :], sems.at[hop, n]
            )
            copy.start()
            copies.append(copy)
    for hop in range(GX):
        head = lax.rem(x + hop, GX) * LOCAL + piece * HP
        rows = meta[...]
        for i in range(HP):
            rows = jnp.where(row == i, gates[head + i].astype(F32), rows)
        small[hop] = jnp.concatenate([rows.astype(BF16)] * HP, 1)
        copy = pltpu.make_async_copy(
            small.at[hop], outs[hop].at[pl.ds(4 * ROWS, 16), :], sems.at[hop, 4]
        )
        copy.start()
        copies.append(copy)
    for copy in copies:
        copy.wait()


def pack(piece, where, q, k, v, dy, gates, meta):
    hbm = pl.BlockSpec(memory_space=pl.ANY)
    return pl.pallas_call(
        lambda *refs: pack_kernel(piece, *refs),
        out_shape=[shape((MESSAGE, WIDE), BF16)] * GX,
        in_specs=[smem()] + [hbm] * 4 + vmem(2),
        out_specs=[hbm] * GX,
        scratch_shapes=[pltpu.VMEM((GX, 16, WIDE), BF16), pltpu.SemaphoreType.DMA((GX, 5))],
        **params(0, 2 * MIB),
        name="pack",
    )(where, q, k, v, dy, gates, meta)


def token_weights(buf):
    mask_rows, weight_rows, gate_rows = [], [], []
    row = lax.broadcasted_iota(jnp.int32, (8, DK), 0)
    for j in range(GX):
        small = buf[j, 4 * ROWS : MESSAGE, 0:DK].astype(F32)
        first, second = small[8:9], small[9:10]
        first_weight, second_weight = small[10:11], small[11:12]
        kind = row.astype(F32)
        hit_first = (kind == first).astype(F32)
        hit_second = (kind == second).astype(F32)
        mask = jnp.where(row < MEMS, hit_first + hit_second, (row == MEMS).astype(F32))
        weight = jnp.where(
            row < MEMS,
            hit_first * first_weight + hit_second * second_weight,
            (row == MEMS).astype(F32),
        )
        for h in range(HP):
            mask_rows.append(mask)
            weight_rows.append(weight)
            gate_rows.append(mask * small[h : h + 1])
    return tuple(jnp.concatenate(r, 0) for r in (mask_rows, weight_rows, gate_rows))


def triangle():
    t = lax.broadcasted_iota(jnp.int32, (DK, DK), 0)
    s = lax.broadcasted_iota(jnp.int32, (DK, DK), 1)
    return t, s


def order_tokens(x, buf, messages):
    for hop in range(GX):
        buf[lax.rem(x + GX - hop, GX)] = messages[hop][...]


def states_kernel(scale, where, m0, m1, m2, m3, o0, o1, o2, o3, buf, acc):
    x, y = where[0], where[1]
    order_tokens(x, buf, (m0, m1, m2, m3))
    mask, weight, gate = token_weights(buf)
    t, s = triangle()
    gate = gate.astype(BF16)
    upper = (t <= s).astype(BF16)
    running = mm(gate, upper)
    total = mm(gate, jnp.ones((DK, DK), BF16))
    size = HP * 8
    part = lambda a, j: a[j * size : (j + 1) * size]
    write_rows, read_rows = [], []
    for j in range(GX):
        later = sum([part(total, i) for i in range(j + 1, GX)], part(total, j))
        before = sum([part(total, i) for i in range(j)], jnp.zeros((size, DK), F32))
        write_rows.append(part(mask, j) * jnp.exp(later - part(running, j)))
        read_rows.append(part(weight, j) * scale * jnp.exp(before + part(running, j)))
    for h in range(HP):
        lanes = slice(h * DK, (h + 1) * DK)
        for side, (left, right, rows) in enumerate(((1, 2, write_rows), (0, 3, read_rows))):
            sums = None
            for j in range(GX):
                turned = buf[j, left * ROWS : (left + 1) * ROWS, lanes].astype(F32).T
                stacked = jnp.concatenate(
                    [(turned * rows[j][h * 8 + e : h * 8 + e + 1]).astype(BF16) for e in range(KINDS)], 0
                )
                term = mm(stacked, buf[j, right * ROWS : (right + 1) * ROWS, lanes])
                sums = term if sums is None else sums + term
            acc[side, h] = sums.reshape(KINDS, DK, DK).astype(BF16)
    for hop, out in enumerate((o0, o1, o2, o3)):
        there = lax.rem(y + hop, GY)
        out[...] = acc[:, :, :, pl.ds(pl.multiple_of(there * PART, PART), PART), :]


def states(scale, where, messages):
    return pl.pallas_call(
        lambda *refs: states_kernel(scale, *refs),
        out_shape=[shape(STATE, BF16)] * GY,
        in_specs=[smem()] + vmem(GX),
        out_specs=vmem(GY),
        scratch_shapes=[
            pltpu.VMEM((GX, MESSAGE, WIDE), BF16),
            pltpu.VMEM((2, HP, KINDS, DK, DK), BF16),
        ],
        **params(600_000_000 * HP, 2 * MIB),
        name="states",
    )(where, *messages)


TS, TG, BTW, MINE, SIB, TABLE = 0, 4, 8, 24, 32, 40


def column(piece, h, e):
    return (piece * HP + h) * 8 + e


def group_kernel(piece, where, table, s0, s1, s2, s3, own, z1, z2, z3):
    y, z = where[1], where[2]
    parts = (s0, s1, s2, s3)
    for h in range(HP):
        for e in range(KINDS):
            col = column(piece, h, e)
            both = []
            for side, base in ((0, TS), (1, TG)):
                acc = jnp.zeros((PART, DK), F32)
                for hop in range(GY):
                    source = lax.rem(y + GY - hop, GY)
                    acc = acc + table[base + source, col] * parts[hop][side, h, e].astype(F32)
                own[side, h, e] = acc
                both.append(acc)
            for hop, out in ((1, z1), (2, z2), (3, z3)):
                ahead = (z + hop < GZ).astype(F32)
                out[h, e] = (ahead * both[0] + (1.0 - ahead) * both[1]).astype(BF16)


def group(piece, where, table, parts):
    return pl.pallas_call(
        lambda *refs: group_kernel(piece, *refs),
        out_shape=[shape(STATE, F32)] + [shape(HALF, BF16)] * 3,
        in_specs=[smem(), smem()] + vmem(GY),
        out_specs=vmem(4),
        **params(10_000_000, 2 * MIB),
        name="group",
    )(where, table, *parts)


def across_kernel(piece, where, table, own, z1, z2, z3, mine, sib):
    z, c = where[2], where[3]
    first = (c == 0).astype(F32)
    for h in range(HP):
        for e in range(KINDS):
            col = column(piece, h, e)
            to_mine = [jnp.zeros((PART, DK), F32)] * 2
            to_sib = [first * own[0, h, e], (1.0 - first) * own[1, h, e]]
            for hop, ref in ((1, z1), (2, z2), (3, z3)):
                source = lax.rem(z + GZ - hop, GZ)
                ahead = (source < z).astype(F32)
                block = ref[h, e].astype(F32)
                near = table[MINE + source * 2 + c, col]
                far = table[SIB + source * 2 + c, col]
                for side, keep in ((0, ahead), (1, 1.0 - ahead)):
                    to_mine[side] = to_mine[side] + (near * keep) * block
                    to_sib[side] = to_sib[side] + (far * keep) * block
            for side in range(2):
                mine[side, h, e] = to_mine[side]
                sib[side, h, e] = to_sib[side].astype(BF16)


def across(piece, where, table, own, arrived):
    return pl.pallas_call(
        lambda *refs: across_kernel(piece, *refs),
        out_shape=[shape(STATE, F32), shape(STATE, BF16)],
        in_specs=[smem(), smem()] + vmem(4),
        out_specs=vmem(2),
        **params(10_000_000, 2 * MIB),
        name="across",
    )(where, table, own, *arrived)


def entering_kernel(piece, where, table, mine, sib, s0, s1, s2, s3, o0, o1, o2, o3):
    y = where[1]
    parts = (s0, s1, s2, s3)
    for h in range(HP):
        for e in range(KINDS):
            col = column(piece, h, e)
            for side, base in ((0, TG), (1, TS)):
                start = mine[side, h, e] + sib[side, h, e].astype(F32)
                blocks = [p[side, h, e].astype(F32) for p in parts]
                for hop, out in enumerate((o0, o1, o2, o3)):
                    there = lax.rem(y + hop, GY)
                    acc = table[base + there, col] * start
                    for back in range(GY):
                        source = lax.rem(y + GY - back, GY)
                        counts = (source < there) if side == 0 else (source > there)
                        factor = table[BTW + source * GY + there, col] * counts.astype(F32)
                        acc = acc + factor * blocks[back]
                    out[side, h, e] = acc.astype(BF16)


def entering(piece, where, table, mine, sib, parts):
    return pl.pallas_call(
        lambda *refs: entering_kernel(piece, *refs),
        out_shape=[shape(STATE, BF16)] * GY,
        in_specs=[smem(), smem()] + vmem(6),
        out_specs=vmem(GY),
        **params(20_000_000, 2 * MIB),
        name="entering",
    )(where, table, mine, sib, *parts)


def spread(block, cols, r):
    return [(block * cols[:, r + e : r + e + 1]).astype(BF16) for e in range(KINDS)]


def within_kernel(scale, where, m0, m1, m2, m3, res, buf, state, late):
    x = where[0]
    order_tokens(x, buf, (m0, m1, m2, m3))
    mask, weight, gate = token_weights(buf)
    t, s = triangle()
    gate = gate.astype(BF16)
    lower = t >= s
    eye = (t == s).astype(BF16)
    ones = jnp.ones((DK, DK), BF16)
    running = mm(gate, (t <= s).astype(BF16))
    total = mm(gate, ones)
    decay = jnp.exp(total)
    write_row = mask * jnp.exp(total - running)
    read_row = weight * scale * jnp.exp(running)
    barred = jnp.where(mask > 0, running, BIG)
    running_col = mm(lower.astype(BF16), gate, NT)
    total_col = mm(ones, gate, NT)
    weight_col = mm(eye, weight.astype(BF16), NT) * scale
    mask_col = mm(eye, mask.astype(BF16), NT)
    read_col = weight_col * jnp.exp(running_col)
    write_col = mask_col * jnp.exp(total_col - running_col)

    for h in range(HP):
        lanes = slice(h * DK, (h + 1) * DK)
        for j in range(GX):
            r = (j * HP + h) * 8
            q, k, v, dy = (buf[j, n * ROWS : (n + 1) * ROWS, lanes] for n in range(4))
            near = jnp.zeros((DK, DK), F32)
            for e in range(KINDS):
                near = near + weight_col[:, r + e : r + e + 1] * jnp.exp(
                    running_col[:, r + e : r + e + 1] - barred[r + e : r + e + 1]
                )
            near = jnp.where(lower, near, 0.0)
            scores = (mm(q, k, NT) * near).astype(BF16)
            grads = (mm(dy, v, NT) * near).astype(BF16)
            out = mm(scores, v)
            grad_q = mm(grads, k)
            if j > 0:
                half = state[0, h].astype(BF16)
                wide = jnp.concatenate(spread(q.astype(F32), read_col, r), 1)
                out = out + mm(wide, half.reshape(KINDS * DK, DK))
                for e, block in enumerate(spread(dy.astype(F32), read_col, r)):
                    grad_q = grad_q + mm(block, half[e], NT)
            res[j, 0:ROWS, lanes] = out.astype(BF16)
            res[j, ROWS : 2 * ROWS, lanes] = grad_q.astype(BF16)
            late[j, h, 0] = mm(grads, q, TN)
            late[j, h, 1] = mm(scores, dy, TN)
            if j < GX - 1:
                turned = k.astype(F32).T
                for e in range(KINDS):
                    grown = mm((turned * write_row[r + e : r + e + 1]).astype(BF16), v)
                    if j > 0:
                        grown = grown + decay[r + e : r + e + 1] * state[0, h, e]
                    state[0, h, e] = grown
        for j in range(GX - 1, -1, -1):
            r = (j * HP + h) * 8
            q, k, v, dy = (buf[j, n * ROWS : (n + 1) * ROWS, lanes] for n in range(4))
            grad_k = late[j, h, 0]
            grad_v = late[j, h, 1]
            if j < GX - 1:
                half = state[1, h].astype(BF16)
                wide = jnp.concatenate(spread(k.astype(F32), write_col, r), 1)
                grad_v = grad_v + mm(wide, half.reshape(KINDS * DK, DK))
                for e, block in enumerate(spread(v.astype(F32), write_col, r)):
                    grad_k = grad_k + mm(block, half[e], NT)
            res[j, 2 * ROWS : 3 * ROWS, lanes] = grad_k.astype(BF16)
            res[j, 3 * ROWS : 4 * ROWS, lanes] = grad_v.astype(BF16)
            if j > 0:
                turned = q.astype(F32).T
                for e in range(KINDS):
                    grown = mm((turned * read_row[r + e : r + e + 1]).astype(BF16), dy)
                    if j < GX - 1:
                        grown = grown + decay[r + e : r + e + 1] * state[1, h, e]
                    state[1, h, e] = grown


def within(scale, where, messages):
    return pl.pallas_call(
        lambda *refs: within_kernel(scale, *refs),
        out_shape=shape((GX, 4 * ROWS, WIDE), BF16),
        in_specs=[smem()] + vmem(GX),
        out_specs=pl.BlockSpec(memory_space=pltpu.VMEM),
        scratch_shapes=[
            pltpu.VMEM((GX, MESSAGE, WIDE), BF16),
            pltpu.VMEM((2, HP, KINDS, DK, DK), F32),
            pltpu.VMEM((GX, HP, 2, DK, DK), F32),
        ],
        **params(1_000_000_000 * HP, 4 * MIB),
        name="within",
    )(where, *messages)


def finish_kernel(scale, where, m0, m1, m2, m3, p0, p1, p2, p3, part, o0, o1, o2, o3, buf, state, res):
    x, y = where[0], where[1]
    order_tokens(x, buf, (m0, m1, m2, m3))
    for hop, ref in enumerate((p0, p1, p2, p3)):
        source = lax.rem(y + GY - hop, GY)
        state[:, :, :, pl.ds(pl.multiple_of(source * PART, PART), PART), :] = ref[...]
    mask, weight, gate = token_weights(buf)
    t, s = triangle()
    gate = gate.astype(BF16)
    eye = (t == s).astype(BF16)
    ones = jnp.ones((DK, DK), BF16)
    running = mm((t >= s).astype(BF16), gate, NT)
    total = mm(ones, gate, NT)
    size = HP * 8
    cut = lambda a, j: a[:, j * size : (j + 1) * size]
    zero = jnp.zeros((DK, size), F32)
    before = jnp.concatenate([sum([cut(total, i) for i in range(j)], zero) for j in range(GX)], 1)
    after = jnp.concatenate([sum([cut(total, i) for i in range(j, GX)], zero) for j in range(GX)], 1)
    read_col = mm(eye, weight.astype(BF16), NT) * scale * jnp.exp(before + running)
    write_col = mm(eye, mask.astype(BF16), NT) * jnp.exp(after - running)
    for h in range(HP):
        lanes = slice(h * DK, (h + 1) * DK)
        for j in range(GX):
            r = (j * HP + h) * 8
            q, k, v, dy = (buf[j, n * ROWS : (n + 1) * ROWS, lanes].astype(F32) for n in range(4))
            for n, source, side, cols, dims in (
                (0, q, 0, read_col, NN),
                (1, dy, 0, read_col, NT),
                (2, v, 1, write_col, NT),
                (3, k, 1, write_col, NN),
            ):
                rows = slice(n * ROWS, (n + 1) * ROWS)
                acc = part[j, rows, lanes].astype(F32)
                blocks = spread(source, cols, r)
                if dims is NN:
                    acc = acc + mm(jnp.concatenate(blocks, 1), state[side, h].reshape(KINDS * DK, DK))
                else:
                    for e, block in enumerate(blocks):
                        acc = acc + mm(block, state[side, h, e], NT)
                res[j, rows, lanes] = acc.astype(BF16)
    for hop, out in enumerate((o0, o1, o2, o3)):
        out[...] = res[lax.rem(x + hop, GX)]


def finish(scale, where, messages, prefixes, part):
    return pl.pallas_call(
        lambda *refs: finish_kernel(scale, *refs),
        out_shape=[shape((4 * ROWS, WIDE), BF16)] * GX,
        in_specs=[smem()] + vmem(GX + GY + 1),
        out_specs=vmem(GX),
        scratch_shapes=[
            pltpu.VMEM((GX, MESSAGE, WIDE), BF16),
            pltpu.VMEM((2, HP, KINDS, DK, DK), BF16),
            pltpu.VMEM((GX, 4 * ROWS, WIDE), BF16),
        ],
        **params(600_000_000 * HP, 4 * MIB),
        name="finish",
    )(where, *messages, *prefixes, part)


def unpack_kernel(piece, where, *refs):
    x = where[0]
    arrived, outs, sems = refs[:GX], refs[-5:-1], refs[-1]
    copies = []
    for hop in range(GX):
        head = lax.rem(x + GX - hop, GX) * LOCAL + piece * HP
        lanes = pl.ds(pl.multiple_of(head * DK, DK), WIDE)
        for n in range(4):
            copy = pltpu.make_async_copy(
                arrived[hop].at[pl.ds(n * ROWS, ROWS), :], outs[n].at[0, :, lanes], sems.at[hop, n]
            )
            copy.start()
            copies.append(copy)
    for copy in copies:
        copy.wait()


def unpack(piece, where, arrived, outputs):
    hbm = pl.BlockSpec(memory_space=pl.ANY)
    return pl.pallas_call(
        lambda *refs: unpack_kernel(piece, *refs),
        out_shape=[shape((1, ROWS, H * DK), BF16)] * 4,
        in_specs=[smem()] + [hbm] * (GX + len(outputs)),
        out_specs=[hbm] * 4,
        scratch_shapes=[pltpu.SemaphoreType.DMA((GX, 4))],
        input_output_aliases={1 + GX + i: i for i in range(len(outputs))},
        **params(0, 2 * MIB),
        name="unpack",
    )(where, *arrived, *outputs)


def shift(array, axis, hop, count, stride=1):
    pairs = [(i, (i + hop * stride) % count) for i in range(count)]
    return lax.ppermute(array, axis, pairs)


def placed(stack, index):
    count = stack.shape[0]
    order = (index - jnp.arange(count)) % count
    return jnp.where((order[:, None] == jnp.arange(count)[None, :])[:, :, None], stack[None], 0.0).sum(1)


def ring(value, axis, count, stride=1):
    return jnp.stack([value] + [shift(value, axis, hop, count * stride, stride) for hop in range(1, count)])


def decay_table(log_decay, chosen, x, y, seqi):
    names = (chosen[:, :, None] == jnp.arange(MEMS)[None, None, :]).any(1).astype(F32)
    masks = jnp.concatenate([names, jnp.ones((ROWS, 1), F32), jnp.zeros((ROWS, 3), F32)], 1)
    sums = (log_decay[:, 0, :].astype(F32)[:, :, None] * masks[None]).sum(1)
    block = ring(sums.reshape(1, H * 8), "mem", GX).sum(0)
    block = lax.dynamic_slice_in_dim(block, x * LOCAL * 8, LOCAL * 8, 1)
    near = placed(ring(block[0], "seqo", GY), y)
    zone = near.sum(0)
    other = lax.ppermute(zone, "seqi", [(i, i ^ 1) for i in range(2 * GZ)])
    pair = jnp.where(seqi % 2 == 0, jnp.concatenate([zone, other]), jnp.concatenate([other, zone]))
    zones = placed(ring(pair, "seqi", GZ, 2), seqi // 2).reshape(2 * GZ, LOCAL * 8)
    terms = jnp.concatenate([near, zones], 0)
    a = jnp.arange(GY)
    pair = jnp.arange(GY * GY)
    i = jnp.arange(2 * GZ)
    sib = jnp.where(seqi % 2 == 0, seqi + 1, seqi - 1)
    low = jnp.concatenate(
        [a, a * 0 - 1, jnp.minimum(pair // GY, pair % GY), jnp.minimum(i, seqi) + GY, jnp.minimum(i, sib) + GY]
    )
    high = jnp.concatenate(
        [a * 0 + GY, a, jnp.maximum(pair // GY, pair % GY), jnp.maximum(i, seqi) + GY, jnp.maximum(i, sib) + GY]
    )
    place = jnp.arange(GY + 2 * GZ)[None, :]
    between = (low[:, None] < place) & (place < high[:, None])
    return jnp.exp(jnp.where(between[:, :, None], terms[None], 0.0).sum(1))


def body(queries, keys, values, log_decay, routes, route_logits, cotangent):
    scale = 2.0 / math.sqrt(DK * ROWS * GX * GY * GZ * 2)
    x, y, seqi = lax.axis_index("mem"), lax.axis_index("seqo"), lax.axis_index("seqi")
    where = jnp.stack([x, y, seqi // 2, seqi % 2]).astype(jnp.int32)
    logits = route_logits[0].astype(F32)
    margin = logits[:, 0] - logits[:, 1]
    named = routes[0].astype(F32)
    meta = jnp.concatenate(
        [
            jnp.zeros((8, ROWS), F32),
            named.T,
            jax.nn.sigmoid(margin)[None],
            jax.nn.sigmoid(-margin)[None],
            jnp.zeros((4, ROWS), F32),
        ],
        0,
    )
    messages = []
    for piece in range(PIECES):
        own = pack(piece, where, queries, keys, values, cotangent, log_decay, meta)
        if piece > 0:
            own, _ = lax.optimization_barrier((own, messages[-1]))
        messages.append([own[0]] + [shift(own[hop], "mem", hop, GX) for hop in range(1, GX)])
    table = decay_table(log_decay, routes[0], x, y, seqi)
    outputs = ()
    for piece in range(PIECES):
        sent = states(scale, where, messages[piece])
        parts = [sent[0]] + [shift(sent[hop], "seqo", hop, GY) for hop in range(1, GY)]
        own, *ahead = group(piece, where, table, parts)
        arrived = [shift(ahead[hop - 1], "seqi", hop, 2 * GZ, 2) for hop in range(1, GZ)]
        mine, sib = across(piece, where, table, own, arrived)
        sib = lax.ppermute(sib, "seqi", [(i, i ^ 1) for i in range(2 * GZ)])
        starts = entering(piece, where, table, mine, sib, parts)
        prefixes = [starts[0]] + [shift(starts[hop], "seqo", hop, GY) for hop in range(1, GY)]
        part = within(scale, where, messages[piece])
        results = finish(scale, where, messages[piece], prefixes, part)
        returned = [results[0]] + [shift(results[hop], "mem", hop, GX) for hop in range(1, GX)]
        outputs = unpack(piece, where, returned, outputs)
    return tuple(outputs)


def solution(mesh):
    tokens = P(("seqi", "seqo"), "mem", None)
    return jax.shard_map(
        body,
        mesh=mesh,
        in_specs=(tokens, tokens, tokens, P(None, ("seqi", "seqo"), "mem"), tokens, tokens, tokens),
        out_specs=(tokens,) * 4,
        check_vma=False,
    )
```

```python
import math

import jax
import jax.numpy as jnp
from jax import lax
from jax.experimental import pallas as pl
from jax.experimental.pallas import tpu as pltpu
from jax.sharding import PartitionSpec as P

H = 16
DK = 128
ROWS = 128
MEMS = 4
KINDS = MEMS + 1
GX = 4
GY = 4
GZ = 4
CHUNKS = GX * GY
GROUP = 4
MESSAGE = 4 * ROWS + 16
DEEP = KINDS * DK
STATE = DEEP + 16
ZONES = 2 * GZ
OTHERS = ZONES - 1
BIG = 1e30
F32 = jnp.float32
BF16 = jnp.bfloat16
MIB = 1 << 20

NT = (((1,), (1,)), ((), ()))
TN = (((0,), (0,)), ((), ()))
NN = (((1,), (0,)), ((), ()))


def mm(a, b, dims=NN):
    return lax.dot_general(a, b, dims, preferred_element_type=F32)


VMEM = pl.BlockSpec(memory_space=pltpu.VMEM)
SMEM = pl.BlockSpec(memory_space=pltpu.SMEM)
HBM = pl.BlockSpec(memory_space=pltpu.HBM)


def params(flops, moved, grant=40 * MIB):
    return dict(
        compiler_params=pltpu.CompilerParams(vmem_limit_bytes=grant),
        cost_estimate=pl.CostEstimate(flops=flops, bytes_accessed=moved, transcendentals=0),
    )


def shape(dims, dtype):
    return jax.ShapeDtypeStruct(dims, dtype)


def pack_kernel(q, k, v, dy, gates, named, logits, out, held, stage, in_sems, out_sems):
    loads = [pltpu.make_async_copy(ref.at[0], held.at[n], in_sems.at[n]) for n, ref in enumerate((q, k, v, dy))]
    for load in loads:
        load.start()
    row = lax.broadcasted_iota(jnp.int32, (16, DK), 0)
    kinds = named[...].astype(F32)
    scores = logits[...].astype(F32)
    margin = scores[0:1] - scores[1:2]
    meta = jnp.zeros((16, DK), F32)
    for place, value in (
        (8, kinds[0:1]),
        (9, kinds[1:2]),
        (10, jax.nn.sigmoid(margin)),
        (11, jax.nn.sigmoid(-margin)),
    ):
        meta = jnp.where(row == place, value, meta)
    rates = gates[...].astype(F32)
    for h in range(H):
        stage[h, 4 * ROWS : MESSAGE, :] = jnp.where(row == 0, rates[h : h + 1], meta).astype(BF16)
    stores = []
    for n, load in enumerate(loads):
        load.wait()
        for h in range(H):
            stage[h, n * ROWS : (n + 1) * ROWS, :] = held[n, :, h * DK : (h + 1) * DK]
        last = ROWS + 16 if n == 3 else ROWS
        part = pl.ds(n * ROWS, last)
        store = pltpu.make_async_copy(stage.at[:, part, :], out.at[:, part, :], out_sems.at[n])
        store.start()
        stores.append(store)
    for store in stores:
        store.wait()


def pack(q, k, v, dy, gates, named, logits):
    return pl.pallas_call(
        pack_kernel,
        out_shape=shape((CHUNKS, MESSAGE, DK), BF16),
        in_specs=[HBM] * 4 + [VMEM] * 3,
        out_specs=HBM,
        scratch_shapes=[
            pltpu.VMEM((4, ROWS, H * DK), BF16),
            pltpu.VMEM((CHUNKS, MESSAGE, DK), BF16),
            pltpu.SemaphoreType.DMA((4,)),
            pltpu.SemaphoreType.DMA((4,)),
        ],
        **params(0, 4 * MIB, 60 * MIB),
        name="pack",
    )(q, k, v, dy, gates, named, logits)


def token_rows(buf):
    mask_rows, weight_rows, gate_rows = [], [], []
    row = lax.broadcasted_iota(jnp.int32, (8, DK), 0)
    kind = row.astype(F32)
    shared = (row == MEMS).astype(F32)
    for j in range(CHUNKS):
        small = buf[j, 4 * ROWS : MESSAGE, :].astype(F32)
        hit_first = jnp.where(row < MEMS, (kind == small[8:9]).astype(F32), 0.0)
        hit_second = jnp.where(row < MEMS, (kind == small[9:10]).astype(F32), 0.0)
        mask = hit_first + hit_second + shared
        mask_rows.append(mask)
        weight_rows.append(hit_first * small[10:11] + hit_second * small[11:12] + shared)
        gate_rows.append(mask * small[0:1])
    mask, weight, gate = (jnp.concatenate(r, 0) for r in (mask_rows, weight_rows, gate_rows))
    t = lax.broadcasted_iota(jnp.int32, (DK, DK), 0)
    s = lax.broadcasted_iota(jnp.int32, (DK, DK), 1)
    gate = gate.astype(BF16)
    running = mm(gate, (t <= s).astype(BF16))
    total = mm(gate, jnp.ones((DK, DK), BF16))
    return mask, weight, running, total


def piled(total):
    parts = [total[8 * j : 8 * j + 8] for j in range(CHUNKS)]
    before, after = [jnp.zeros((8, DK), F32)], [parts[-1]]
    for j in range(CHUNKS - 1):
        before.append(before[-1] + parts[j])
        after.append(after[-1] + parts[CHUNKS - 2 - j])
    return jnp.concatenate(before, 0), jnp.concatenate(after[::-1], 0)


def row_block(rows, r):
    few = jnp.broadcast_to(rows[r : r + 1], (16, DK)).astype(BF16)
    return jnp.concatenate([few] * (DK // 16), 0)


def col_block(cols, r):
    return jnp.broadcast_to(cols[:, r : r + 1], (DK, DK)).astype(BF16)


def tokens(buf, j):
    return (buf[j, n * ROWS : (n + 1) * ROWS, :] for n in range(4))


def states_kernel(scale, where, buf, *refs):
    outs, wide = refs[:OTHERS], refs[OTHERS]
    mask, weight, running, total = token_rows(buf)
    before, after = piled(total)
    write_rows = mask * jnp.exp(after - running)
    read_rows = weight * scale * jnp.exp(before + running)
    both = []
    for side, (left, right, rows) in enumerate(((1, 2, write_rows), (0, 3, read_rows))):
        for j in range(CHUNKS):
            turned = buf[j, left * ROWS : (left + 1) * ROWS, :].T
            for e in range(KINDS):
                wide[side, e * DK : (e + 1) * DK, j * DK : (j + 1) * DK] = turned * row_block(rows, j * 8 + e)
        facing = jnp.concatenate([buf[j, right * ROWS : (right + 1) * ROWS, :] for j in range(CHUNKS)], 0)
        sums = mm(wide[side], facing)
        both.append(sums.astype(BF16))
    coarse = after[0:8].astype(BF16).astype(F32)
    length = jnp.concatenate([coarse, after[0:8] - coarse], 0).astype(BF16)
    for hop, out in enumerate(outs, 1):
        later = where[0] + hop < 2 * GZ
        out[DEEP:STATE, :] = length

        @pl.when(later)
        def _():
            out[0:DEEP, :] = both[0]

        @pl.when(jnp.logical_not(later))
        def _():
            out[0:DEEP, :] = both[1]


def states(scale, where, messages):
    return pl.pallas_call(
        lambda *refs: states_kernel(scale, *refs),
        out_shape=[shape((STATE, DK), BF16)] * OTHERS,
        in_specs=[SMEM, VMEM],
        out_specs=[VMEM] * OTHERS,
        scratch_shapes=[pltpu.VMEM((2, DEEP, CHUNKS * DK), BF16)],
        **params(700_000_000, 4 * MIB),
        name="states",
    )(where, messages)


def within_kernel(scale, buf, res, state):
    mask, weight, running, total = token_rows(buf)
    t = lax.broadcasted_iota(jnp.int32, (DK, DK), 0)
    s = lax.broadcasted_iota(jnp.int32, (DK, DK), 1)
    lower = t >= s
    decay = jnp.exp(total)
    write_row = mask * jnp.exp(total - running)
    read_row = weight * scale * jnp.exp(running)
    barred = jnp.where(mask > 0, running, BIG)
    running_col = running.T
    weight_col = (weight * scale).T
    read_col = read_row.T
    write_col = write_row.T
    for j in range(CHUNKS):
        q, k, v, dy = tokens(buf, j)
        near = jnp.zeros((DK, DK), F32)
        for r in range(j * 8, j * 8 + KINDS):
            near = near + weight_col[:, r : r + 1] * jnp.exp(running_col[:, r : r + 1] - barred[r : r + 1])
        near = jnp.where(lower, near, 0.0)
        scores = (mm(q, k, NT) * near).astype(BF16)
        grads = (mm(dy, v, NT) * near).astype(BF16)
        res[j, 0] = mm(scores, v)
        res[j, 1] = mm(grads, k)
        res[j, 2] = mm(grads, q, TN)
        res[j, 3] = mm(scores, dy, TN)

    def step(side, j, start, last, cols, rows, places):
        left, right, cross = places
        blocks = list(tokens(buf, j))
        a, b = blocks[left], blocks[right]
        if not start:
            spread = [col_block(cols, j * 8 + e) for e in range(KINDS)]
            half = state[side].astype(BF16)
            res[j, 2 if side else 0] += sum(
                [mm((b if side else a) * spread[e], half[e * DK : (e + 1) * DK], NT if side else NN) for e in range(KINDS)]
            )
            res[j, 3 if side else 1] += sum(
                [mm((a if side else b) * spread[e], half[e * DK : (e + 1) * DK], NN if side else NT) for e in range(KINDS)]
            )
        if not last:
            grow, face = blocks[cross[0]].T, blocks[cross[1]]
            for e in range(KINDS):
                part = slice(e * DK, (e + 1) * DK)
                grown = mm(grow * row_block(rows, j * 8 + e), face)
                if not start:
                    grown = grown + decay[j * 8 + e : j * 8 + e + 1] * state[side, part, :]
                state[side, part, :] = grown

    for i in range(CHUNKS):
        step(0, i, i == 0, i == CHUNKS - 1, read_col, write_row, (0, 3, (1, 2)))
        back = CHUNKS - 1 - i
        step(1, back, i == 0, i == CHUNKS - 1, write_col, read_row, (1, 2, (0, 3)))


def within(scale, messages):
    return pl.pallas_call(
        lambda *refs: within_kernel(scale, *refs),
        out_shape=shape((CHUNKS, 4, ROWS, DK), F32),
        in_specs=[VMEM],
        out_specs=VMEM,
        scratch_shapes=[pltpu.VMEM((2, DEEP, DK), F32)],
        **params(2_000_000_000, 6 * MIB),
        name="within",
    )(messages)


def entering(mine, total, arrived, lengths):
    lengths[mine] = total
    sources = [lax.rem(mine + ZONES - hop, ZONES) for hop in range(1, ZONES)]
    for source, ref in zip(sources, arrived):
        tail = ref[DEEP:STATE, :].astype(F32)
        lengths[source] = tail[0:8] + tail[8:16]
    start = [jnp.zeros((DEEP, DK), F32), jnp.zeros((DEEP, DK), F32)]
    for source, ref in zip(sources, arrived):
        low, high = jnp.minimum(source, mine), jnp.maximum(source, mine)
        gap = jnp.zeros((8, DK), F32)
        for zone in range(ZONES):
            inside = jnp.logical_and(low < zone, zone < high).astype(F32)
            gap = gap + inside * lengths[zone]
        factor = jnp.exp(gap)
        earlier = (source < mine).astype(F32)
        block = ref[0:DEEP, :].astype(F32).reshape(KINDS, DK, DK) * factor[0:KINDS].reshape(KINDS, 1, DK)
        block = block.reshape(DEEP, DK)
        start[0] = start[0] + earlier * block
        start[1] = start[1] + (1.0 - earlier) * block
    return [side.astype(BF16) for side in start]


def turned(state):
    return jnp.concatenate([state[e * DK : (e + 1) * DK].T for e in range(KINDS)], 0)


def finish_kernel(scale, where, buf, part, *refs):
    arrived, out, lengths = refs[:OTHERS], refs[OTHERS], refs[OTHERS + 1]
    mask, weight, running, total = token_rows(buf)
    before, after = piled(total)
    read_col = (weight * scale * jnp.exp(before + running)).T
    write_col = (mask * jnp.exp(after - running)).T
    state = entering(where[0], after[0:8], arrived, lengths)
    flipped = [turned(s) for s in state]
    for first in range(0, CHUNKS, GROUP):
        group = range(first, first + GROUP)
        blocks = [list(tokens(buf, j)) for j in group]
        for cols, jobs in (
            (read_col, ((0, state[0]), (3, flipped[0]))),
            (write_col, ((1, state[1]), (2, flipped[1]))),
        ):
            spread = [[col_block(cols, j * 8 + e) for e in range(KINDS)] for j in group]
            for source, right in jobs:
                left = jnp.concatenate(
                    [jnp.concatenate([blocks[i][source] * w for w in spread[i]], 1) for i in range(GROUP)], 0
                )
                sums = mm(left, right)
                n = (0, 3, 2, 1)[source]
                for i, j in enumerate(group):
                    out[j, n * ROWS : (n + 1) * ROWS, :] = (
                        part[j, n] + sums[i * ROWS : (i + 1) * ROWS]
                    ).astype(BF16)


def finish(scale, where, messages, part, arrived):
    return pl.pallas_call(
        lambda *refs: finish_kernel(scale, *refs),
        out_shape=shape((CHUNKS, 4 * ROWS, DK), BF16),
        in_specs=[SMEM] + [VMEM] * (2 + OTHERS),
        out_specs=VMEM,
        scratch_shapes=[pltpu.VMEM((ZONES, 8, DK), F32)],
        **params(1_300_000_000, 8 * MIB),
        name="finish",
    )(where, messages, part, *arrived)


def unpack_kernel(arrived, *refs):
    outs, stage, sems = refs[:4], refs[4], refs[5]
    stores = []
    for n, out in enumerate(outs):
        for h in range(H):
            stage[n, :, h * DK : (h + 1) * DK] = arrived[h, n * ROWS : (n + 1) * ROWS, :]
        store = pltpu.make_async_copy(stage.at[n], out.at[0], sems.at[n])
        store.start()
        stores.append(store)
    for store in stores:
        store.wait()


def unpack(arrived):
    return pl.pallas_call(
        unpack_kernel,
        out_shape=[shape((1, ROWS, H * DK), BF16)] * 4,
        in_specs=[VMEM],
        out_specs=[HBM] * 4,
        scratch_shapes=[pltpu.VMEM((4, ROWS, H * DK), BF16), pltpu.SemaphoreType.DMA((4,))],
        **params(0, 4 * MIB),
        name="unpack",
    )(arrived)


def body(queries, keys, values, log_decay, routes, route_logits, cotangent):
    scale = 2.0 / math.sqrt(DK * ROWS * GX * GY * ZONES)
    where = lax.axis_index("seqi").astype(jnp.int32).reshape(1)
    packed = pack(queries, keys, values, cotangent, log_decay[:, 0, :], routes[0].T, route_logits[0].T)
    messages = lax.all_to_all(packed, ("seqo", "mem"), 0, 0, tiled=True)
    sent = states(scale, where, messages)
    arrived = [
        lax.ppermute(block, "seqi", [(i, (i + hop) % ZONES) for i in range(ZONES)])
        for hop, block in enumerate(sent, 1)
    ]
    part = within(scale, messages)
    results = finish(scale, where, messages, part, arrived)
    returned = lax.all_to_all(results, ("seqo", "mem"), 0, 0, tiled=True)
    return tuple(unpack(returned))


def solution(mesh):
    tokens_spec = P(("seqi", "seqo"), "mem", None)
    return jax.shard_map(
        body,
        mesh=mesh,
        in_specs=(tokens_spec,) * 3 + (P(None, ("seqi", "seqo"), "mem"),) + (tokens_spec,) * 3,
        out_specs=(tokens_spec,) * 4,
        check_vma=False,
    )
```

```python
import math

import jax
import jax.numpy as jnp
from jax import lax
from jax.experimental import pallas as pl
from jax.experimental.pallas import tpu as pltpu
from jax.sharding import PartitionSpec as P

H = 16
DK = 128
ROWS = 128
MEMS = 4
KINDS = MEMS + 1
GX = 4
GY = 4
GZ = 4
CHUNKS = GX * GY
GROUP = 4
GROUPS = CHUNKS // GROUP
MESSAGE = 4 * ROWS + 16
DEEP = KINDS * DK
STATE = DEEP + 16
ZONES = 2 * GZ
OTHERS = GZ
BIG = 1e30
F32 = jnp.float32
BF16 = jnp.bfloat16
MIB = 1 << 20

NT = (((1,), (1,)), ((), ()))
TN = (((0,), (0,)), ((), ()))
NN = (((1,), (0,)), ((), ()))


def mm(a, b, dims=NN):
    return lax.dot_general(a, b, dims, preferred_element_type=F32)


VMEM = pl.BlockSpec(memory_space=pltpu.VMEM)
HBM = pl.BlockSpec(memory_space=pltpu.HBM)


def params(flops, moved, grant=20 * MIB):
    return dict(
        compiler_params=pltpu.CompilerParams(vmem_limit_bytes=grant),
        cost_estimate=pl.CostEstimate(flops=flops, bytes_accessed=moved, transcendentals=0),
    )


def shape(dims, dtype):
    return jax.ShapeDtypeStruct(dims, dtype)


def pack_kernel(q, k, v, dy, *refs):
    small, (out, held, stage, gates, named, logits, in_sems, out_sems) = refs[:3], refs[3:]
    fetches = [
        pltpu.make_async_copy(ref, place, in_sems.at[4 + n])
        for n, (ref, place) in enumerate(zip(small, (gates, named, logits)))
    ]
    for fetch in fetches:
        fetch.start()
    loads = [pltpu.make_async_copy(ref.at[0], held.at[n], in_sems.at[n]) for n, ref in enumerate((q, k, v, dy))]
    for load in loads:
        load.start()
    for fetch in fetches:
        fetch.wait()
    row = lax.broadcasted_iota(jnp.int32, (16, DK), 0)
    kinds = named[...].astype(F32)
    scores = logits[...].astype(F32)
    margin = scores[0:1] - scores[1:2]
    meta = jnp.zeros((16, DK), F32)
    for place, value in (
        (8, kinds[0:1]),
        (9, kinds[1:2]),
        (10, jax.nn.sigmoid(margin)),
        (11, jax.nn.sigmoid(-margin)),
    ):
        meta = jnp.where(row == place, value, meta)
    rates = gates[...].astype(F32)
    for h in range(H):
        stage[h, 4 * ROWS : MESSAGE, :] = jnp.where(row == 0, rates[h : h + 1], meta).astype(BF16)
    stores = []
    for n, load in enumerate(loads):
        load.wait()
        for h in range(H):
            stage[h, n * ROWS : (n + 1) * ROWS, :] = held[n, :, h * DK : (h + 1) * DK]
        last = ROWS + 16 if n == 3 else ROWS
        part = pl.ds(n * ROWS, last)
        store = pltpu.make_async_copy(stage.at[:, part, :], out.at[:, part, :], out_sems.at[n])
        store.start()
        stores.append(store)
    for store in stores:
        store.wait()


def pack(q, k, v, dy, gates, named, logits):
    return pl.pallas_call(
        pack_kernel,
        out_shape=shape((CHUNKS, MESSAGE, DK), BF16),
        in_specs=[HBM] * 7,
        out_specs=HBM,
        scratch_shapes=[
            pltpu.VMEM((4, ROWS, H * DK), BF16),
            pltpu.VMEM((CHUNKS, MESSAGE, DK), BF16),
            pltpu.VMEM((H, DK), BF16),
            pltpu.VMEM((2, DK), jnp.int32),
            pltpu.VMEM((2, DK), BF16),
            pltpu.SemaphoreType.DMA((7,)),
            pltpu.SemaphoreType.DMA((4,)),
        ],
        **params(0, 4 * MIB, 60 * MIB),
        name="pack",
    )(q, k, v, dy, gates, named, logits)


def kind_rows(first, second, first_weight, second_weight):
    row = lax.broadcasted_iota(jnp.int32, (8, DK), 0)
    kind = row.astype(F32)
    shared = (row == MEMS).astype(F32)
    hit_first = jnp.where(row < MEMS, (kind == first).astype(F32), 0.0)
    hit_second = jnp.where(row < MEMS, (kind == second).astype(F32), 0.0)
    return hit_first + hit_second + shared, hit_first * first_weight + hit_second * second_weight + shared


def running_sums(gate):
    t = lax.broadcasted_iota(jnp.int32, (DK, DK), 0)
    s = lax.broadcasted_iota(jnp.int32, (DK, DK), 1)
    gate = gate.astype(BF16)
    return mm(gate, (t <= s).astype(BF16)), mm(gate, jnp.ones((DK, DK), BF16))


def token_rows(buf):
    mask_rows, weight_rows, gate_rows = [], [], []
    for j in range(CHUNKS):
        small = buf[j, 4 * ROWS : MESSAGE, :].astype(F32)
        mask, weight = kind_rows(small[8:9], small[9:10], small[10:11], small[11:12])
        mask_rows.append(mask)
        weight_rows.append(weight)
        gate_rows.append(mask * small[0:1])
    mask, weight, gate = (jnp.concatenate(r, 0) for r in (mask_rows, weight_rows, gate_rows))
    return (mask, weight) + running_sums(gate)


def piled(total):
    parts = [total[8 * j : 8 * j + 8] for j in range(CHUNKS)]
    before, after, whole = [], [], []
    for first in range(0, CHUNKS, GROUP):
        group = parts[first : first + GROUP]
        ahead, behind = [jnp.zeros((8, DK), F32)], [group[-1]]
        for j in range(GROUP - 1):
            ahead.append(ahead[-1] + group[j])
            behind.append(behind[-1] + group[GROUP - 2 - j])
        before += ahead
        after += behind[::-1]
        whole.append(behind[-1])
    return jnp.concatenate(before, 0), jnp.concatenate(after, 0), whole


def by_kind(rows, block):
    return (block.reshape(KINDS, DK, DK) * rows[0:KINDS].reshape(KINDS, 1, DK)).reshape(DEEP, DK)


def row_block(rows, r):
    few = jnp.broadcast_to(rows[r : r + 1], (16, DK)).astype(BF16)
    return jnp.concatenate([few] * (DK // 16), 0)


def col_block(cols, r):
    return jnp.broadcast_to(cols[:, r : r + 1], (DK, DK)).astype(BF16)


def tokens(buf, j):
    return (buf[j, n * ROWS : (n + 1) * ROWS, :] for n in range(4))


def states_kernel(scale, buf, local, *refs):
    mine = lax.axis_index("seqi")
    outs, wide = refs[:OTHERS], refs[OTHERS]
    mask, weight, running, total = token_rows(buf)
    before, after, whole = piled(total)
    write_rows = mask * jnp.exp(after - running)
    read_rows = weight * scale * jnp.exp(before + running)
    decay = [jnp.exp(w) for w in whole]
    both = []
    for side, (left, right, rows) in enumerate(((1, 2, write_rows), (0, 3, read_rows))):
        sums = jnp.zeros((DEEP, DK), F32)
        for g in range(GROUPS) if side == 0 else range(GROUPS - 1, -1, -1):
            local[side, g] = sums.astype(BF16)
            group = range(g * GROUP, (g + 1) * GROUP)
            for j in group:
                flipped = buf[j, left * ROWS : (left + 1) * ROWS, :].T
                for e in range(KINDS):
                    wide[side, e * DK : (e + 1) * DK, j * DK : (j + 1) * DK] = flipped * row_block(rows, j * 8 + e)
            facing = jnp.concatenate([buf[j, right * ROWS : (right + 1) * ROWS, :] for j in group], 0)
            grown = mm(wide[side, :, g * GROUP * DK : (g + 1) * GROUP * DK], facing)
            sums = by_kind(decay[g], sums) + grown
        both.append(sums.astype(BF16))
    zone = sum(whole[1:], whole[0])
    coarse = zone.astype(BF16).astype(F32)
    length = jnp.concatenate([coarse, zone - coarse], 0).astype(BF16)
    for hop, out in enumerate(outs):
        z, c = mine // 2, mine % 2
        later = z + hop < GZ if hop > 0 else c == 0
        out[DEEP:STATE, :] = length

        @pl.when(later)
        def _():
            out[0:DEEP, :] = both[0]

        @pl.when(jnp.logical_not(later))
        def _():
            out[0:DEEP, :] = both[1]


def states(scale, messages):
    return pl.pallas_call(
        lambda *refs: states_kernel(scale, *refs),
        out_shape=[shape((2, GROUPS, DEEP, DK), BF16)] + [shape((STATE, DK), BF16)] * OTHERS,
        in_specs=[VMEM],
        out_specs=[VMEM] * (1 + OTHERS),
        scratch_shapes=[pltpu.VMEM((2, DEEP, CHUNKS * DK), BF16)],
        **params(700_000_000, 4 * MIB),
        name="states",
    )(messages)


def split(rows):
    coarse = rows.astype(BF16).astype(F32)
    return coarse, rows - coarse


def cross_kernel(scale, buf, res):
    mask, weight, running, total = token_rows(buf)
    write_row = mask * jnp.exp(total - running)
    read_row = weight * scale * jnp.exp(running)
    part = lambda a, j: a[8 * j : 8 * j + 8]
    barred = jnp.where(mask > 0, running, BIG)
    running_col = running.T
    weight_col = (weight * scale).T
    t = lax.broadcasted_iota(jnp.int32, (DK, DK), 0)
    lower = t >= lax.broadcasted_iota(jnp.int32, (DK, DK), 1)
    for g in range(GROUPS):
        first = g * GROUP
        last = first + GROUP
        sums = {}

        def add(j, n, value):
            sums[j, n] = sums[j, n] + value if (j, n) in sums else value

        for j in range(first, last):
            q, k, v, dy = tokens(buf, j)
            rows = range(j, last)
            later = range(j + 1, last)
            stack = lambda n: jnp.concatenate([buf[i, n * ROWS : (n + 1) * ROWS, :] for i in rows], 0)
            decay = jnp.zeros((DK, DK), F32)
            for r in range(j * 8, j * 8 + KINDS):
                decay = decay + weight_col[:, r : r + 1] * jnp.exp(running_col[:, r : r + 1] - barred[r : r + 1])
            decay = jnp.where(lower, decay, 0.0)
            reads, gap = [], jnp.zeros((8, DK), F32)
            for i in later:
                coarse, fine = split(part(read_row, i) * jnp.exp(gap))
                reads.append(jnp.concatenate([coarse, fine, coarse, jnp.zeros((8, DK), F32)], 0))
                gap = gap + part(total, i)
            if reads:
                coarse, fine = split(part(write_row, j))
                writes = jnp.concatenate([coarse, coarse, fine, jnp.zeros((8, DK), F32)], 0).astype(BF16)
                below = mm(jnp.concatenate(reads, 1).astype(BF16), writes, TN)
                decay = jnp.concatenate([decay, below], 0)
            queries, cotangents = stack(0), stack(3)
            attend = (mm(queries, k, NT) * decay).astype(BF16)
            grads = (mm(cotangents, v, NT) * decay).astype(BF16)
            out, grad_q = mm(attend, v), mm(grads, k)
            for place, i in enumerate(rows):
                add(i, 0, out[place * ROWS : (place + 1) * ROWS])
                add(i, 1, grad_q[place * ROWS : (place + 1) * ROWS])
            add(j, 2, mm(grads, queries, TN))
            add(j, 3, mm(attend, cotangents, TN))
        for (j, n), value in sums.items():
            res[j, n] = value


def cross(scale, messages):
    return pl.pallas_call(
        lambda *refs: cross_kernel(scale, *refs),
        out_shape=shape((CHUNKS, 4, ROWS, DK), F32),
        in_specs=[VMEM],
        out_specs=VMEM,
        **params(2_000_000_000, 6 * MIB),
        name="cross",
    )(messages)


def entering(mine, zone, arrived, lengths):
    z, c = mine // 2, mine % 2
    lengths[mine] = zone
    sources = [lax.rem(z + GZ - hop, GZ) * 2 + c for hop in range(1, GZ)]
    sources += [lax.rem(z + GZ - hop, GZ) * 2 + 1 - c for hop in range(GZ)]
    for source, ref in zip(sources, arrived):
        tail = ref[DEEP:STATE, :].astype(F32)
        lengths[source] = tail[0:8] + tail[8:16]
    start = [jnp.zeros((DEEP, DK), F32), jnp.zeros((DEEP, DK), F32)]
    for source, ref in zip(sources, arrived):
        low, high = jnp.minimum(source, mine), jnp.maximum(source, mine)
        gap = jnp.zeros((8, DK), F32)
        for other in range(ZONES):
            inside = jnp.logical_and(low < other, other < high).astype(F32)
            gap = gap + inside * lengths[other]
        earlier = (source < mine).astype(F32)
        factor = jnp.exp(gap)
        block = ref[0:DEEP, :].astype(F32)
        start[0] = start[0] + by_kind(factor * earlier, block)
        start[1] = start[1] + by_kind(factor * (1.0 - earlier), block)
    return start


def turned(state):
    return jnp.concatenate([state[e * DK : (e + 1) * DK].T for e in range(KINDS)], 0)


def finish_kernel(scale, buf, part, local, *refs):
    arrived, (out, lengths, stage, sems) = refs[: ZONES - 1], refs[ZONES - 1 :]
    stores = []
    mask, weight, running, total = token_rows(buf)
    before, after, whole = piled(total)
    read_col = (weight * scale * jnp.exp(before + running)).T
    write_col = (mask * jnp.exp(after - running)).T
    start = entering(lax.axis_index("seqi"), sum(whole[1:], whole[0]), arrived, lengths)
    for g in range(GROUPS):
        group = range(g * GROUP, (g + 1) * GROUP)
        ahead = sum(whole[:g], jnp.zeros((8, DK), F32))
        behind = sum(whole[g + 1 :], jnp.zeros((8, DK), F32))
        state = [
            (local[side, g].astype(F32) + by_kind(jnp.exp(gap), start[side])).astype(BF16)
            for side, gap in enumerate((ahead, behind))
        ]
        flipped = [turned(block) for block in state]
        blocks = [list(tokens(buf, j)) for j in group]
        for cols, jobs in (
            (read_col, ((0, state[0]), (3, flipped[0]))),
            (write_col, ((1, state[1]), (2, flipped[1]))),
        ):
            spread = [[col_block(cols, j * 8 + e) for e in range(KINDS)] for j in group]
            for source, right in jobs:
                left = jnp.concatenate(
                    [jnp.concatenate([blocks[i][source] * w for w in spread[i]], 1) for i in range(GROUP)], 0
                )
                sums = mm(left, right)
                n = (0, 3, 2, 1)[source]
                for i, j in enumerate(group):
                    stage[j, n * ROWS : (n + 1) * ROWS, :] = (
                        part[j, n] + sums[i * ROWS : (i + 1) * ROWS]
                    ).astype(BF16)
        rows = pl.ds(g * GROUP, GROUP)
        store = pltpu.make_async_copy(stage.at[rows], out.at[rows], sems.at[g])
        store.start()
        stores.append(store)
    for store in stores:
        store.wait()


def finish(scale, messages, part, local, arrived):
    return pl.pallas_call(
        lambda *refs: finish_kernel(scale, *refs),
        out_shape=shape((CHUNKS, 4 * ROWS, DK), BF16),
        in_specs=[VMEM] * (2 + ZONES),
        out_specs=HBM,
        scratch_shapes=[
            pltpu.VMEM((ZONES, 8, DK), F32),
            pltpu.VMEM((CHUNKS, 4 * ROWS, DK), BF16),
            pltpu.SemaphoreType.DMA((GROUPS,)),
        ],
        **params(1_300_000_000, 8 * MIB),
        name="finish",
    )(messages, part, local, *arrived)


def unpack_kernel(arrived, *refs):
    outs, stage, sems = refs[:4], refs[4], refs[5]
    stores = []
    for n, out in enumerate(outs):
        rows = slice(n * ROWS, (n + 1) * ROWS)
        for h in range(H):
            stage[n, :, h * DK : (h + 1) * DK] = arrived[h, rows, :]
        store = pltpu.make_async_copy(stage.at[n], out.at[0], sems.at[n])
        store.start()
        stores.append(store)
    for store in stores:
        store.wait()


def unpack(arrived):
    return pl.pallas_call(
        unpack_kernel,
        out_shape=[shape((1, ROWS, H * DK), BF16)] * 4,
        in_specs=[VMEM],
        out_specs=[HBM] * 4,
        scratch_shapes=[pltpu.VMEM((4, ROWS, H * DK), BF16), pltpu.SemaphoreType.DMA((4,))],
        **params(0, 4 * MIB),
        name="unpack",
    )(arrived)


def body(queries, keys, values, log_decay, routes, route_logits, cotangent):
    scale = 2.0 / math.sqrt(DK * ROWS * GX * GY * ZONES)
    packed = pack(queries, keys, values, cotangent, log_decay[:, 0, :], routes[0].T, route_logits[0].T)
    messages = lax.all_to_all(packed, ("seqo", "mem"), 0, 0, tiled=True)
    local, to_sibling, *sent = states(scale, messages)
    sibling = [(i, i ^ 1) for i in range(ZONES)]
    arrived = [
        lax.ppermute(block, "seqi", [(i, (i + 2 * hop) % ZONES) for i in range(ZONES)])
        for hop, block in enumerate(sent, 1)
    ]
    beside = [lax.ppermute(to_sibling, "seqi", sibling)]
    part = cross(scale, messages)
    arrived, part = lax.optimization_barrier((arrived, part))
    beside += [lax.ppermute(block, "seqi", sibling) for block in arrived]
    results = finish(scale, messages, part, local, arrived + beside)
    returned = lax.all_to_all(results, ("seqo", "mem"), 0, 0, tiled=True)
    return tuple(unpack(returned))


def solution(mesh):
    tokens_spec = P(("seqi", "seqo"), "mem", None)
    return jax.shard_map(
        body,
        mesh=mesh,
        in_specs=(tokens_spec,) * 3 + (P(None, ("seqi", "seqo"), "mem"),) + (tokens_spec,) * 3,
        out_specs=(tokens_spec,) * 4,
        check_vma=False,
    )
```

```python
import math

import jax
import jax.numpy as jnp
from jax import lax
from jax.experimental import pallas as pl
from jax.experimental.pallas import tpu as pltpu
from jax.sharding import PartitionSpec as P

H = 16
DK = 128
ROWS = 128
MEMS = 4
KINDS = MEMS + 1
GX = 4
GY = 4
GZ = 4
CHUNKS = GX * GY
GROUP = 4
GROUPS = CHUNKS // GROUP
MESSAGE = 4 * ROWS + 16
DEEP = KINDS * DK
STATE = DEEP + 16
ZONES = 2 * GZ
OTHERS = GZ
BIG = 1e30
F32 = jnp.float32
BF16 = jnp.bfloat16
MIB = 1 << 20

NT = (((1,), (1,)), ((), ()))
TN = (((0,), (0,)), ((), ()))
NN = (((1,), (0,)), ((), ()))


def mm(a, b, dims=NN):
    return lax.dot_general(a, b, dims, preferred_element_type=F32)


VMEM = pl.BlockSpec(memory_space=pltpu.VMEM)
HBM = pl.BlockSpec(memory_space=pltpu.HBM)


def params(flops, moved, grant=20 * MIB):
    return dict(
        compiler_params=pltpu.CompilerParams(vmem_limit_bytes=grant),
        cost_estimate=pl.CostEstimate(flops=flops, bytes_accessed=moved, transcendentals=0),
    )


def shape(dims, dtype):
    return jax.ShapeDtypeStruct(dims, dtype)


def pack_kernel(q, k, v, dy, *refs):
    small, (out, held, stage, gates, named, logits, in_sems, out_sems) = refs[:3], refs[3:]
    fetches = [
        pltpu.make_async_copy(ref, place, in_sems.at[4 + n])
        for n, (ref, place) in enumerate(zip(small, (gates, named, logits)))
    ]
    for fetch in fetches:
        fetch.start()
    loads = [pltpu.make_async_copy(ref.at[0], held.at[n], in_sems.at[n]) for n, ref in enumerate((q, k, v, dy))]
    for load in loads:
        load.start()
    for fetch in fetches:
        fetch.wait()
    row = lax.broadcasted_iota(jnp.int32, (16, DK), 0)
    kinds = named[...].astype(F32)
    scores = logits[...].astype(F32)
    margin = scores[0:1] - scores[1:2]
    meta = jnp.zeros((16, DK), F32)
    for place, value in (
        (8, kinds[0:1]),
        (9, kinds[1:2]),
        (10, jax.nn.sigmoid(margin)),
        (11, jax.nn.sigmoid(-margin)),
    ):
        meta = jnp.where(row == place, value, meta)
    rates = gates[...].astype(F32)
    for h in range(H):
        stage[h, 4 * ROWS : MESSAGE, :] = jnp.where(row == 0, rates[h : h + 1], meta).astype(BF16)
    stores = []
    for n, load in enumerate(loads):
        load.wait()
        for h in range(H):
            stage[h, n * ROWS : (n + 1) * ROWS, :] = held[n, :, h * DK : (h + 1) * DK]
        last = ROWS + 16 if n == 3 else ROWS
        part = pl.ds(n * ROWS, last)
        store = pltpu.make_async_copy(stage.at[:, part, :], out.at[:, part, :], out_sems.at[n])
        store.start()
        stores.append(store)
    for store in stores:
        store.wait()


def pack(q, k, v, dy, gates, named, logits):
    return pl.pallas_call(
        pack_kernel,
        out_shape=shape((CHUNKS, MESSAGE, DK), BF16),
        in_specs=[HBM] * 7,
        out_specs=HBM,
        scratch_shapes=[
            pltpu.VMEM((4, ROWS, H * DK), BF16),
            pltpu.VMEM((CHUNKS, MESSAGE, DK), BF16),
            pltpu.VMEM((H, DK), BF16),
            pltpu.VMEM((2, DK), jnp.int32),
            pltpu.VMEM((2, DK), BF16),
            pltpu.SemaphoreType.DMA((7,)),
            pltpu.SemaphoreType.DMA((4,)),
        ],
        **params(0, 4 * MIB, 60 * MIB),
        name="pack",
    )(q, k, v, dy, gates, named, logits)


def kind_rows(first, second, first_weight, second_weight):
    row = lax.broadcasted_iota(jnp.int32, (8, DK), 0)
    kind = row.astype(F32)
    shared = (row == MEMS).astype(F32)
    hit_first = jnp.where(row < MEMS, (kind == first).astype(F32), 0.0)
    hit_second = jnp.where(row < MEMS, (kind == second).astype(F32), 0.0)
    return hit_first + hit_second + shared, hit_first * first_weight + hit_second * second_weight + shared


def running_sums(gate):
    t = lax.broadcasted_iota(jnp.int32, (DK, DK), 0)
    s = lax.broadcasted_iota(jnp.int32, (DK, DK), 1)
    gate = gate.astype(BF16)
    return mm(gate, (t <= s).astype(BF16)), mm(gate, jnp.ones((DK, DK), BF16))


def token_rows(buf):
    mask_rows, weight_rows, gate_rows = [], [], []
    for j in range(CHUNKS):
        small = buf[j, 4 * ROWS : MESSAGE, :].astype(F32)
        mask, weight = kind_rows(small[8:9], small[9:10], small[10:11], small[11:12])
        mask_rows.append(mask)
        weight_rows.append(weight)
        gate_rows.append(mask * small[0:1])
    mask, weight, gate = (jnp.concatenate(r, 0) for r in (mask_rows, weight_rows, gate_rows))
    return (mask, weight) + running_sums(gate)


def piled(total):
    parts = [total[8 * j : 8 * j + 8] for j in range(CHUNKS)]
    before, after, whole = [], [], []
    for first in range(0, CHUNKS, GROUP):
        group = parts[first : first + GROUP]
        ahead, behind = [jnp.zeros((8, DK), F32)], [group[-1]]
        for j in range(GROUP - 1):
            ahead.append(ahead[-1] + group[j])
            behind.append(behind[-1] + group[GROUP - 2 - j])
        before += ahead
        after += behind[::-1]
        whole.append(behind[-1])
    return jnp.concatenate(before, 0), jnp.concatenate(after, 0), whole


def by_kind(rows, block):
    return (block.reshape(KINDS, DK, DK) * rows[0:KINDS].reshape(KINDS, 1, DK)).reshape(DEEP, DK)


def row_block(rows, r):
    few = jnp.broadcast_to(rows[r : r + 1], (16, DK)).astype(BF16)
    return jnp.concatenate([few] * (DK // 16), 0)


def col_block(cols, r):
    return jnp.broadcast_to(cols[:, r : r + 1], (DK, DK)).astype(BF16)


def tokens(buf, j):
    return (buf[j, n * ROWS : (n + 1) * ROWS, :] for n in range(4))


def states_kernel(scale, buf, local, *refs):
    mine = lax.axis_index("seqi")
    outs, wide = refs[:OTHERS], refs[OTHERS]
    mask, weight, running, total = token_rows(buf)
    before, after, whole = piled(total)
    write_rows = mask * jnp.exp(after - running)
    read_rows = weight * scale * jnp.exp(before + running)
    decay = [jnp.exp(w) for w in whole]
    both = []
    for side, (left, right, rows) in enumerate(((1, 2, write_rows), (0, 3, read_rows))):
        sums = jnp.zeros((DEEP, DK), F32)
        for g in range(GROUPS) if side == 0 else range(GROUPS - 1, -1, -1):
            local[side, g] = sums.astype(BF16)
            group = range(g * GROUP, (g + 1) * GROUP)
            for j in group:
                flipped = buf[j, left * ROWS : (left + 1) * ROWS, :].T
                for e in range(KINDS):
                    wide[side, e * DK : (e + 1) * DK, j * DK : (j + 1) * DK] = flipped * row_block(rows, j * 8 + e)
            facing = jnp.concatenate([buf[j, right * ROWS : (right + 1) * ROWS, :] for j in group], 0)
            grown = mm(wide[side, :, g * GROUP * DK : (g + 1) * GROUP * DK], facing)
            sums = by_kind(decay[g], sums) + grown
        both.append(sums.astype(BF16))
    zone = sum(whole[1:], whole[0])
    coarse = zone.astype(BF16).astype(F32)
    length = jnp.concatenate([coarse, zone - coarse], 0).astype(BF16)
    for hop, out in enumerate(outs):
        z, c = mine // 2, mine % 2
        later = z + hop < GZ if hop > 0 else c == 0
        out[DEEP:STATE, :] = length

        @pl.when(later)
        def _():
            out[0:DEEP, :] = both[0]

        @pl.when(jnp.logical_not(later))
        def _():
            out[0:DEEP, :] = both[1]


def states(scale, messages):
    return pl.pallas_call(
        lambda *refs: states_kernel(scale, *refs),
        out_shape=[shape((2, GROUPS, DEEP, DK), BF16)] + [shape((STATE, DK), BF16)] * OTHERS,
        in_specs=[VMEM],
        out_specs=[VMEM] * (1 + OTHERS),
        scratch_shapes=[pltpu.VMEM((2, DEEP, CHUNKS * DK), BF16)],
        **params(700_000_000, 4 * MIB),
        name="states",
    )(messages)


def split(rows):
    coarse = rows.astype(BF16).astype(F32)
    return coarse, rows - coarse


def cross_kernel(scale, buf, res):
    mask, weight, running, total = token_rows(buf)
    write_row = mask * jnp.exp(total - running)
    read_row = weight * scale * jnp.exp(running)
    part = lambda a, j: a[8 * j : 8 * j + 8]
    barred = jnp.where(mask > 0, running, BIG)
    named = weight > 0
    shifted_col = (running + jnp.where(named, jnp.log(jnp.where(named, weight, 1.0) * scale), -BIG)).T
    t = lax.broadcasted_iota(jnp.int32, (DK, DK), 0)
    lower = t >= lax.broadcasted_iota(jnp.int32, (DK, DK), 1)
    def own_decay(j):
        decay = jnp.zeros((DK, DK), F32)
        for r in range(j * 8, j * 8 + KINDS):
            decay = decay + jnp.exp(shifted_col[:, r : r + 1] - barred[r : r + 1])
        return jnp.where(lower, decay, 0.0)

    def factors(early, late):
        reads, writes, gap = [], [], jnp.zeros((8, DK), F32)
        for i in late:
            coarse, fine = split(part(read_row, i) * jnp.exp(gap))
            reads.append(jnp.concatenate([coarse, fine, coarse, jnp.zeros((8, DK), F32)], 0))
            gap = gap + part(total, i)
        gap = jnp.zeros((8, DK), F32)
        for j in early[::-1]:
            coarse, fine = split(part(write_row, j) * jnp.exp(gap))
            writes.insert(0, jnp.concatenate([coarse, coarse, fine, jnp.zeros((8, DK), F32)], 0))
            gap = gap + part(total, j)
        reads, writes = (jnp.concatenate(r, 1).astype(BF16) for r in (reads, writes))
        return mm(reads, writes, TN)

    def tile(add, early, late, decay):
        stack = lambda n, js: jnp.concatenate([buf[j, n * ROWS : (n + 1) * ROWS, :] for j in js], 0)
        q, dy = stack(0, late), stack(3, late)
        k, v = stack(1, early), stack(2, early)
        attend = (mm(q, k, NT) * decay).astype(BF16)
        grads = (mm(dy, v, NT) * decay).astype(BF16)
        for n, js, left, right, dims in (
            (0, late, attend, v, NN),
            (1, late, grads, k, NN),
            (2, early, grads, q, TN),
            (3, early, attend, dy, TN),
        ):
            value = mm(left, right, dims)
            for place, j in enumerate(js):
                add(j, n, value[place * ROWS : (place + 1) * ROWS])

    for g in range(GROUPS):
        first = g * GROUP
        sums = {}

        def add(j, n, value):
            sums[j, n] = sums[j, n] + value if (j, n) in sums else value

        for pair in ((first, first + 1), (first + 2, first + 3)):
            ends = [own_decay(j) for j in pair]
            below = factors(pair[:1], pair[1:])
            empty = jnp.zeros((DK, DK), F32)
            decay = jnp.concatenate(
                [jnp.concatenate([ends[0], empty], 1), jnp.concatenate([below, ends[1]], 1)], 0
            )
            tile(add, pair, pair, decay)
        early, late = (first, first + 1), (first + 2, first + 3)
        tile(add, early, late, factors(early, late))
        for (j, n), value in sums.items():
            res[j, n] = value


def cross(scale, messages):
    return pl.pallas_call(
        lambda *refs: cross_kernel(scale, *refs),
        out_shape=shape((CHUNKS, 4, ROWS, DK), F32),
        in_specs=[VMEM],
        out_specs=VMEM,
        **params(2_000_000_000, 6 * MIB),
        name="cross",
    )(messages)


def entering(mine, zone, arrived, lengths):
    z, c = mine // 2, mine % 2
    lengths[mine] = zone
    sources = [lax.rem(z + GZ - hop, GZ) * 2 + c for hop in range(1, GZ)]
    sources += [lax.rem(z + GZ - hop, GZ) * 2 + 1 - c for hop in range(GZ)]
    for source, ref in zip(sources, arrived):
        tail = ref[DEEP:STATE, :].astype(F32)
        lengths[source] = tail[0:8] + tail[8:16]
    start = [jnp.zeros((DEEP, DK), F32), jnp.zeros((DEEP, DK), F32)]
    for source, ref in zip(sources, arrived):
        low, high = jnp.minimum(source, mine), jnp.maximum(source, mine)
        gap = jnp.zeros((8, DK), F32)
        for other in range(ZONES):
            inside = jnp.logical_and(low < other, other < high).astype(F32)
            gap = gap + inside * lengths[other]
        earlier = (source < mine).astype(F32)
        factor = jnp.exp(gap)
        block = ref[0:DEEP, :].astype(F32)
        start[0] = start[0] + by_kind(factor * earlier, block)
        start[1] = start[1] + by_kind(factor * (1.0 - earlier), block)
    return start


def turned(state):
    return jnp.concatenate([state[e * DK : (e + 1) * DK].T for e in range(KINDS)], 0)


def finish_kernel(scale, buf, part, local, *refs):
    arrived, (out, lengths) = refs[: ZONES - 1], refs[ZONES - 1 :]
    mask, weight, running, total = token_rows(buf)
    before, after, whole = piled(total)
    read_col = (weight * scale * jnp.exp(before + running)).T
    write_col = (mask * jnp.exp(after - running)).T
    start = entering(lax.axis_index("seqi"), sum(whole[1:], whole[0]), arrived, lengths)
    for g in range(GROUPS):
        group = range(g * GROUP, (g + 1) * GROUP)
        ahead = sum(whole[:g], jnp.zeros((8, DK), F32))
        behind = sum(whole[g + 1 :], jnp.zeros((8, DK), F32))
        state = [
            (local[side, g].astype(F32) + by_kind(jnp.exp(gap), start[side])).astype(BF16)
            for side, gap in enumerate((ahead, behind))
        ]
        flipped = [turned(block) for block in state]
        blocks = [list(tokens(buf, j)) for j in group]
        for cols, jobs in (
            (read_col, ((0, state[0]), (3, flipped[0]))),
            (write_col, ((1, state[1]), (2, flipped[1]))),
        ):
            spread = [[col_block(cols, j * 8 + e) for e in range(KINDS)] for j in group]
            for source, right in jobs:
                left = jnp.concatenate(
                    [jnp.concatenate([blocks[i][source] * w for w in spread[i]], 1) for i in range(GROUP)], 0
                )
                sums = mm(left, right)
                n = (0, 3, 2, 1)[source]
                for i, j in enumerate(group):
                    out[j, n * ROWS : (n + 1) * ROWS, :] = (
                        part[j, n] + sums[i * ROWS : (i + 1) * ROWS]
                    ).astype(BF16)


def finish(scale, messages, part, local, arrived):
    return pl.pallas_call(
        lambda *refs: finish_kernel(scale, *refs),
        out_shape=shape((CHUNKS, 4 * ROWS, DK), BF16),
        in_specs=[VMEM] * (2 + ZONES),
        out_specs=VMEM,
        scratch_shapes=[pltpu.VMEM((ZONES, 8, DK), F32)],
        **params(1_300_000_000, 8 * MIB),
        name="finish",
    )(messages, part, local, *arrived)


def unpack_kernel(arrived, *refs):
    outs, stage, sems = refs[:4], refs[4], refs[5]
    stores = []
    for n, out in enumerate(outs):
        rows = slice(n * ROWS, (n + 1) * ROWS)
        for h in range(H):
            stage[n, :, h * DK : (h + 1) * DK] = arrived[h, rows, :]
        store = pltpu.make_async_copy(stage.at[n], out.at[0], sems.at[n])
        store.start()
        stores.append(store)
    for store in stores:
        store.wait()


def unpack(arrived):
    return pl.pallas_call(
        unpack_kernel,
        out_shape=[shape((1, ROWS, H * DK), BF16)] * 4,
        in_specs=[VMEM],
        out_specs=[HBM] * 4,
        scratch_shapes=[pltpu.VMEM((4, ROWS, H * DK), BF16), pltpu.SemaphoreType.DMA((4,))],
        **params(0, 4 * MIB),
        name="unpack",
    )(arrived)


def body(queries, keys, values, log_decay, routes, route_logits, cotangent):
    scale = 2.0 / math.sqrt(DK * ROWS * GX * GY * ZONES)
    packed = pack(queries, keys, values, cotangent, log_decay[:, 0, :], routes[0].T, route_logits[0].T)
    messages = lax.all_to_all(packed, ("seqo", "mem"), 0, 0, tiled=True)
    local, to_sibling, *sent = states(scale, messages)
    sibling = [(i, i ^ 1) for i in range(ZONES)]
    arrived = [
        lax.ppermute(block, "seqi", [(i, (i + 2 * hop) % ZONES) for i in range(ZONES)])
        for hop, block in enumerate(sent, 1)
    ]
    beside = [lax.ppermute(to_sibling, "seqi", sibling)]
    part = cross(scale, messages)
    arrived, part = lax.optimization_barrier((arrived, part))
    beside += [lax.ppermute(block, "seqi", sibling) for block in arrived]
    results = finish(scale, messages, part, local, arrived + beside)
    returned = lax.all_to_all(results, ("seqo", "mem"), 0, 0, tiled=True)
    return tuple(unpack(returned))


def solution(mesh):
    tokens_spec = P(("seqi", "seqo"), "mem", None)
    return jax.shard_map(
        body,
        mesh=mesh,
        in_specs=(tokens_spec,) * 3 + (P(None, ("seqi", "seqo"), "mem"),) + (tokens_spec,) * 3,
        out_specs=(tokens_spec,) * 4,
        check_vma=False,
    )
```

```python
import math

import jax
import jax.numpy as jnp
from jax import lax
from jax.experimental import pallas as pl
from jax.experimental.pallas import tpu as pltpu
from jax.sharding import PartitionSpec as P

H = 16
DK = 128
ROWS = 128
MEMS = 4
KINDS = MEMS + 1
GX = 4
GY = 4
GZ = 4
CHUNKS = GX * GY
GROUP = 4
GROUPS = CHUNKS // GROUP
MESSAGE = 4 * ROWS + 16
DEEP = KINDS * DK
STATE = DEEP + 16
ZONES = 2 * GZ
OTHERS = GZ
BIG = 1e30
F32 = jnp.float32
BF16 = jnp.bfloat16
MIB = 1 << 20

NT = (((1,), (1,)), ((), ()))
TN = (((0,), (0,)), ((), ()))
NN = (((1,), (0,)), ((), ()))


def mm(a, b, dims=NN):
    return lax.dot_general(a, b, dims, preferred_element_type=F32)


VMEM = pl.BlockSpec(memory_space=pltpu.VMEM)
HBM = pl.BlockSpec(memory_space=pltpu.HBM)


def params(flops, moved, grant=20 * MIB):
    return dict(
        compiler_params=pltpu.CompilerParams(vmem_limit_bytes=grant),
        cost_estimate=pl.CostEstimate(flops=flops, bytes_accessed=moved, transcendentals=0),
    )


def shape(dims, dtype):
    return jax.ShapeDtypeStruct(dims, dtype)


def pack_kernel(q, k, v, dy, *refs):
    small, (logits, out, held, stage, gates, named, in_sems, out_sems) = refs[:2], refs[2:]
    fetches = [
        pltpu.make_async_copy(ref, place, in_sems.at[4 + n])
        for n, (ref, place) in enumerate(zip(small, (gates, named)))
    ]
    for fetch in fetches:
        fetch.start()
    loads = [pltpu.make_async_copy(ref.at[0], held.at[n], in_sems.at[n]) for n, ref in enumerate((q, k, v, dy))]
    for load in loads:
        load.start()
    for fetch in fetches:
        fetch.wait()
    row = lax.broadcasted_iota(jnp.int32, (16, DK), 0)
    kinds = named[...].astype(F32)
    scores = logits[...].astype(F32)
    margin = scores[0:1] - scores[1:2]
    meta = jnp.zeros((16, DK), F32)
    for place, value in (
        (8, kinds[0:1]),
        (9, kinds[1:2]),
        (10, jax.nn.sigmoid(margin)),
        (11, jax.nn.sigmoid(-margin)),
    ):
        meta = jnp.where(row == place, value, meta)
    rates = gates[...].astype(F32)
    for h in range(H):
        stage[h, 4 * ROWS : MESSAGE, :] = jnp.where(row == 0, rates[h : h + 1], meta).astype(BF16)
    stores = []
    for n, load in enumerate(loads):
        load.wait()
        for h in range(H):
            stage[h, n * ROWS : (n + 1) * ROWS, :] = held[n, :, h * DK : (h + 1) * DK]
        last = ROWS + 16 if n == 3 else ROWS
        part = pl.ds(n * ROWS, last)
        store = pltpu.make_async_copy(stage.at[:, part, :], out.at[:, part, :], out_sems.at[n])
        store.start()
        stores.append(store)
    for store in stores:
        store.wait()


def pack(q, k, v, dy, gates, named, logits):
    return pl.pallas_call(
        pack_kernel,
        out_shape=shape((CHUNKS, MESSAGE, DK), BF16),
        in_specs=[HBM] * 6 + [VMEM],
        out_specs=HBM,
        scratch_shapes=[
            pltpu.VMEM((4, ROWS, H * DK), BF16),
            pltpu.VMEM((CHUNKS, MESSAGE, DK), BF16),
            pltpu.VMEM((H, DK), BF16),
            pltpu.VMEM((2, DK), jnp.int32),
            pltpu.SemaphoreType.DMA((6,)),
            pltpu.SemaphoreType.DMA((4,)),
        ],
        **params(0, 4 * MIB, 60 * MIB),
        name="pack",
    )(q, k, v, dy, gates, named, logits)


def kind_rows(first, second, first_weight, second_weight):
    row = lax.broadcasted_iota(jnp.int32, (8, DK), 0)
    kind = row.astype(F32)
    shared = (row == MEMS).astype(F32)
    hit_first = jnp.where(row < MEMS, (kind == first).astype(F32), 0.0)
    hit_second = jnp.where(row < MEMS, (kind == second).astype(F32), 0.0)
    return hit_first + hit_second + shared, hit_first * first_weight + hit_second * second_weight + shared


def running_sums(gate):
    t = lax.broadcasted_iota(jnp.int32, (DK, DK), 0)
    s = lax.broadcasted_iota(jnp.int32, (DK, DK), 1)
    gate = gate.astype(BF16)
    return mm(gate, (t <= s).astype(BF16)), mm(gate, jnp.ones((DK, DK), BF16))


def token_rows(buf):
    mask_rows, weight_rows, gate_rows = [], [], []
    for j in range(CHUNKS):
        small = buf[j, 4 * ROWS : MESSAGE, :].astype(F32)
        mask, weight = kind_rows(small[8:9], small[9:10], small[10:11], small[11:12])
        mask_rows.append(mask)
        weight_rows.append(weight)
        gate_rows.append(mask * small[0:1])
    mask, weight, gate = (jnp.concatenate(r, 0) for r in (mask_rows, weight_rows, gate_rows))
    return (mask, weight) + running_sums(gate)


def piled(total):
    parts = [total[8 * j : 8 * j + 8] for j in range(CHUNKS)]
    before, after, whole = [], [], []
    for first in range(0, CHUNKS, GROUP):
        group = parts[first : first + GROUP]
        ahead, behind = [jnp.zeros((8, DK), F32)], [group[-1]]
        for j in range(GROUP - 1):
            ahead.append(ahead[-1] + group[j])
            behind.append(behind[-1] + group[GROUP - 2 - j])
        before += ahead
        after += behind[::-1]
        whole.append(behind[-1])
    return jnp.concatenate(before, 0), jnp.concatenate(after, 0), whole


def by_kind(rows, block):
    return (block.reshape(KINDS, DK, DK) * rows[0:KINDS].reshape(KINDS, 1, DK)).reshape(DEEP, DK)


def row_block(rows, r):
    few = jnp.broadcast_to(rows[r : r + 1], (16, DK)).astype(BF16)
    return jnp.concatenate([few] * (DK // 16), 0)


def col_block(cols, r):
    return jnp.broadcast_to(cols[:, r : r + 1], (DK, DK)).astype(BF16)


def tokens(buf, j):
    return (buf[j, n * ROWS : (n + 1) * ROWS, :] for n in range(4))


def states_kernel(scale, buf, local, *refs):
    mine = lax.axis_index("seqi")
    outs, wide = refs[:OTHERS], refs[OTHERS]
    mask, weight, running, total = token_rows(buf)
    before, after, whole = piled(total)
    write_rows = mask * jnp.exp(after - running)
    read_rows = weight * scale * jnp.exp(before + running)
    decay = [jnp.exp(w) for w in whole]
    both = []
    for side, (left, right, rows) in enumerate(((1, 2, write_rows), (0, 3, read_rows))):
        sums = jnp.zeros((DEEP, DK), F32)
        for g in range(GROUPS) if side == 0 else range(GROUPS - 1, -1, -1):
            local[side, g] = sums.astype(BF16)
            group = range(g * GROUP, (g + 1) * GROUP)
            for j in group:
                flipped = buf[j, left * ROWS : (left + 1) * ROWS, :].T
                for e in range(KINDS):
                    wide[side, e * DK : (e + 1) * DK, j * DK : (j + 1) * DK] = flipped * row_block(rows, j * 8 + e)
            facing = jnp.concatenate([buf[j, right * ROWS : (right + 1) * ROWS, :] for j in group], 0)
            grown = mm(wide[side, :, g * GROUP * DK : (g + 1) * GROUP * DK], facing)
            sums = by_kind(decay[g], sums) + grown
        both.append(sums.astype(BF16))
    zone = sum(whole[1:], whole[0])
    coarse = zone.astype(BF16).astype(F32)
    length = jnp.concatenate([coarse, zone - coarse], 0).astype(BF16)
    for hop, out in enumerate(outs):
        z, c = mine // 2, mine % 2
        later = z + hop < GZ if hop > 0 else c == 0
        out[DEEP:STATE, :] = length

        @pl.when(later)
        def _():
            out[0:DEEP, :] = both[0]

        @pl.when(jnp.logical_not(later))
        def _():
            out[0:DEEP, :] = both[1]


def states(scale, messages):
    return pl.pallas_call(
        lambda *refs: states_kernel(scale, *refs),
        out_shape=[shape((2, GROUPS, DEEP, DK), BF16)] + [shape((STATE, DK), BF16)] * OTHERS,
        in_specs=[VMEM],
        out_specs=[VMEM] * (1 + OTHERS),
        scratch_shapes=[pltpu.VMEM((2, DEEP, CHUNKS * DK), BF16)],
        **params(700_000_000, 4 * MIB),
        name="states",
    )(messages)


def split(rows):
    coarse = rows.astype(BF16).astype(F32)
    return coarse, rows - coarse


def cross_kernel(scale, buf, res):
    mask, weight, running, total = token_rows(buf)
    write_row = mask * jnp.exp(total - running)
    read_row = weight * scale * jnp.exp(running)
    part = lambda a, j: a[8 * j : 8 * j + 8]
    barred = jnp.where(mask > 0, running, BIG)
    named = weight > 0
    shifted_col = (running + jnp.where(named, jnp.log(jnp.where(named, weight, 1.0) * scale), -BIG)).T
    t = lax.broadcasted_iota(jnp.int32, (DK, DK), 0)
    lower = t >= lax.broadcasted_iota(jnp.int32, (DK, DK), 1)
    def own_decay(j):
        decay = jnp.zeros((DK, DK), F32)
        for r in range(j * 8, j * 8 + KINDS):
            decay = decay + jnp.exp(shifted_col[:, r : r + 1] - barred[r : r + 1])
        return jnp.where(lower, decay, 0.0)

    def factors(early, late):
        reads, writes, gap = [], [], jnp.zeros((8, DK), F32)
        for i in late:
            coarse, fine = split(part(read_row, i) * jnp.exp(gap))
            reads.append(jnp.concatenate([coarse, fine, coarse, jnp.zeros((8, DK), F32)], 0))
            gap = gap + part(total, i)
        gap = jnp.zeros((8, DK), F32)
        for j in early[::-1]:
            coarse, fine = split(part(write_row, j) * jnp.exp(gap))
            writes.insert(0, jnp.concatenate([coarse, coarse, fine, jnp.zeros((8, DK), F32)], 0))
            gap = gap + part(total, j)
        reads, writes = (jnp.concatenate(r, 1).astype(BF16) for r in (reads, writes))
        return mm(reads, writes, TN)

    def tile(add, early, late, decay):
        stack = lambda n, js: jnp.concatenate([buf[j, n * ROWS : (n + 1) * ROWS, :] for j in js], 0)
        q, dy = stack(0, late), stack(3, late)
        k, v = stack(1, early), stack(2, early)
        attend = (mm(q, k, NT) * decay).astype(BF16)
        grads = (mm(dy, v, NT) * decay).astype(BF16)
        for n, js, left, right, dims in (
            (0, late, attend, v, NN),
            (1, late, grads, k, NN),
            (2, early, grads, q, TN),
            (3, early, attend, dy, TN),
        ):
            value = mm(left, right, dims)
            for place, j in enumerate(js):
                add(j, n, value[place * ROWS : (place + 1) * ROWS])

    for g in range(GROUPS):
        first = g * GROUP
        sums = {}

        def add(j, n, value):
            sums[j, n] = sums[j, n] + value if (j, n) in sums else value

        for pair in ((first, first + 1), (first + 2, first + 3)):
            ends = [own_decay(j) for j in pair]
            below = factors(pair[:1], pair[1:])
            empty = jnp.zeros((DK, DK), F32)
            decay = jnp.concatenate(
                [jnp.concatenate([ends[0], empty], 1), jnp.concatenate([below, ends[1]], 1)], 0
            )
            tile(add, pair, pair, decay)
        early, late = (first, first + 1), (first + 2, first + 3)
        tile(add, early, late, factors(early, late))
        for (j, n), value in sums.items():
            res[j, n] = value


def cross(scale, messages):
    return pl.pallas_call(
        lambda *refs: cross_kernel(scale, *refs),
        out_shape=shape((CHUNKS, 4, ROWS, DK), F32),
        in_specs=[VMEM],
        out_specs=VMEM,
        **params(2_000_000_000, 6 * MIB),
        name="cross",
    )(messages)


def entering(mine, zone, arrived, lengths):
    z, c = mine // 2, mine % 2
    lengths[mine] = zone
    sources = [lax.rem(z + GZ - hop, GZ) * 2 + c for hop in range(1, GZ)]
    sources += [lax.rem(z + GZ - hop, GZ) * 2 + 1 - c for hop in range(GZ)]
    for source, ref in zip(sources, arrived):
        tail = ref[DEEP:STATE, :].astype(F32)
        lengths[source] = tail[0:8] + tail[8:16]
    start = [jnp.zeros((DEEP, DK), F32), jnp.zeros((DEEP, DK), F32)]
    for source, ref in zip(sources, arrived):
        low, high = jnp.minimum(source, mine), jnp.maximum(source, mine)
        gap = jnp.zeros((8, DK), F32)
        for other in range(ZONES):
            inside = jnp.logical_and(low < other, other < high).astype(F32)
            gap = gap + inside * lengths[other]
        earlier = (source < mine).astype(F32)
        factor = jnp.exp(gap)
        block = ref[0:DEEP, :].astype(F32)
        start[0] = start[0] + by_kind(factor * earlier, block)
        start[1] = start[1] + by_kind(factor * (1.0 - earlier), block)
    return start


def turned(state):
    return jnp.concatenate([state[e * DK : (e + 1) * DK].T for e in range(KINDS)], 0)


def finish_kernel(scale, buf, part, local, *refs):
    arrived, (out, lengths) = refs[: ZONES - 1], refs[ZONES - 1 :]
    mask, weight, running, total = token_rows(buf)
    before, after, whole = piled(total)
    read_col = (weight * scale * jnp.exp(before + running)).T
    write_col = (mask * jnp.exp(after - running)).T
    start = entering(lax.axis_index("seqi"), sum(whole[1:], whole[0]), arrived, lengths)
    for g in range(GROUPS):
        group = range(g * GROUP, (g + 1) * GROUP)
        ahead = sum(whole[:g], jnp.zeros((8, DK), F32))
        behind = sum(whole[g + 1 :], jnp.zeros((8, DK), F32))
        state = [
            (local[side, g].astype(F32) + by_kind(jnp.exp(gap), start[side])).astype(BF16)
            for side, gap in enumerate((ahead, behind))
        ]
        flipped = [turned(block) for block in state]
        blocks = [list(tokens(buf, j)) for j in group]
        for cols, jobs in (
            (read_col, ((0, state[0]), (3, flipped[0]))),
            (write_col, ((1, state[1]), (2, flipped[1]))),
        ):
            spread = [[col_block(cols, j * 8 + e) for e in range(KINDS)] for j in group]
            for source, right in jobs:
                n = (0, 3, 2, 1)[source]
                sums = jnp.concatenate([part[j, n] for j in group], 0)
                for e in range(KINDS):
                    left = jnp.concatenate([blocks[i][source] * spread[i][e] for i in range(GROUP)], 0)
                    sums = sums + mm(left, right[e * DK : (e + 1) * DK])
                for i, j in enumerate(group):
                    out[j, n * ROWS : (n + 1) * ROWS, :] = sums[i * ROWS : (i + 1) * ROWS].astype(BF16)


def finish(scale, messages, part, local, arrived):
    return pl.pallas_call(
        lambda *refs: finish_kernel(scale, *refs),
        out_shape=shape((CHUNKS, 4 * ROWS, DK), BF16),
        in_specs=[VMEM] * (2 + ZONES),
        out_specs=VMEM,
        scratch_shapes=[pltpu.VMEM((ZONES, 8, DK), F32)],
        **params(1_300_000_000, 8 * MIB),
        name="finish",
    )(messages, part, local, *arrived)


def unpack_kernel(arrived, *refs):
    outs, stage, sems = refs[:4], refs[4], refs[5]
    stores = []
    for n, out in enumerate(outs):
        rows = slice(n * ROWS, (n + 1) * ROWS)
        for h in range(H):
            stage[n, :, h * DK : (h + 1) * DK] = arrived[h, rows, :]
        store = pltpu.make_async_copy(stage.at[n], out.at[0], sems.at[n])
        store.start()
        stores.append(store)
    for store in stores:
        store.wait()


def unpack(arrived):
    return pl.pallas_call(
        unpack_kernel,
        out_shape=[shape((1, ROWS, H * DK), BF16)] * 4,
        in_specs=[VMEM],
        out_specs=[HBM] * 4,
        scratch_shapes=[pltpu.VMEM((4, ROWS, H * DK), BF16), pltpu.SemaphoreType.DMA((4,))],
        **params(0, 4 * MIB),
        name="unpack",
    )(arrived)


def body(queries, keys, values, log_decay, routes, route_logits, cotangent):
    scale = 2.0 / math.sqrt(DK * ROWS * GX * GY * ZONES)
    packed = pack(queries, keys, values, cotangent, log_decay[:, 0, :], routes[0].T, route_logits[0].T)
    messages = lax.all_to_all(packed, ("seqo", "mem"), 0, 0, tiled=True)
    local, to_sibling, *sent = states(scale, messages)
    sibling = [(i, i ^ 1) for i in range(ZONES)]
    arrived = [
        lax.ppermute(block, "seqi", [(i, (i + 2 * hop) % ZONES) for i in range(ZONES)])
        for hop, block in enumerate(sent, 1)
    ]
    beside = [lax.ppermute(to_sibling, "seqi", sibling)]
    part = cross(scale, messages)
    arrived, part = lax.optimization_barrier((arrived, part))
    beside += [lax.ppermute(block, "seqi", sibling) for block in arrived]
    results = finish(scale, messages, part, local, arrived + beside)
    returned = lax.all_to_all(results, ("seqo", "mem"), 0, 0, tiled=True)
    return tuple(unpack(returned))


def solution(mesh):
    tokens_spec = P(("seqi", "seqo"), "mem", None)
    return jax.shard_map(
        body,
        mesh=mesh,
        in_specs=(tokens_spec,) * 3 + (P(None, ("seqi", "seqo"), "mem"),) + (tokens_spec,) * 3,
        out_specs=(tokens_spec,) * 4,
        check_vma=False,
    )
```

```python
import math

import jax
import jax.numpy as jnp
from jax import lax
from jax.experimental import pallas as pl
from jax.experimental.pallas import tpu as pltpu
from jax.sharding import PartitionSpec as P

H = 16
DK = 128
ROWS = 128
MEMS = 4
KINDS = MEMS + 1
GX = 4
GY = 4
GZ = 4
CHUNKS = GX * GY
GROUP = 4
GROUPS = CHUNKS // GROUP
SOONER = CHUNKS - GROUP
MESSAGE = 4 * ROWS + 16
DEEP = KINDS * DK
STATE = DEEP + 16
ZONES = 2 * GZ
OTHERS = GZ
BIG = 1e30
F32 = jnp.float32
BF16 = jnp.bfloat16
MIB = 1 << 20

NT = (((1,), (1,)), ((), ()))
TN = (((0,), (0,)), ((), ()))
NN = (((1,), (0,)), ((), ()))


def mm(a, b, dims=NN):
    return lax.dot_general(a, b, dims, preferred_element_type=F32)


VMEM = pl.BlockSpec(memory_space=pltpu.VMEM)
HBM = pl.BlockSpec(memory_space=pltpu.HBM)


def params(flops, moved, grant=20 * MIB):
    return dict(
        compiler_params=pltpu.CompilerParams(vmem_limit_bytes=grant),
        cost_estimate=pl.CostEstimate(flops=flops, bytes_accessed=moved, transcendentals=0),
    )


def shape(dims, dtype):
    return jax.ShapeDtypeStruct(dims, dtype)


def pack_kernel(q, k, v, dy, *refs):
    small, (logits, out, held, stage, gates, named, in_sems, out_sems) = refs[:2], refs[2:]
    fetches = [
        pltpu.make_async_copy(ref, place, in_sems.at[4 + n])
        for n, (ref, place) in enumerate(zip(small, (gates, named)))
    ]
    for fetch in fetches:
        fetch.start()
    loads = [pltpu.make_async_copy(ref.at[0], held.at[n], in_sems.at[n]) for n, ref in enumerate((q, k, v, dy))]
    for load in loads:
        load.start()
    for fetch in fetches:
        fetch.wait()
    row = lax.broadcasted_iota(jnp.int32, (16, DK), 0)
    kinds = named[...].astype(F32)
    scores = logits[...].astype(F32)
    margin = scores[0:1] - scores[1:2]
    meta = jnp.zeros((16, DK), F32)
    for place, value in (
        (8, kinds[0:1]),
        (9, kinds[1:2]),
        (10, jax.nn.sigmoid(margin)),
        (11, jax.nn.sigmoid(-margin)),
    ):
        meta = jnp.where(row == place, value, meta)
    rates = gates[...].astype(F32)
    for h in range(H):
        stage[h, 4 * ROWS : MESSAGE, :] = jnp.where(row == 0, rates[h : h + 1], meta).astype(BF16)
    stores = []
    for n, load in enumerate(loads):
        load.wait()
        for h in range(H):
            stage[h, n * ROWS : (n + 1) * ROWS, :] = held[n, :, h * DK : (h + 1) * DK]
        last = ROWS + 16 if n == 3 else ROWS
        part = pl.ds(n * ROWS, last)
        store = pltpu.make_async_copy(stage.at[:, part, :], out.at[:, part, :], out_sems.at[n])
        store.start()
        stores.append(store)
    for store in stores:
        store.wait()


def pack(q, k, v, dy, gates, named, logits):
    return pl.pallas_call(
        pack_kernel,
        out_shape=shape((CHUNKS, MESSAGE, DK), BF16),
        in_specs=[HBM] * 6 + [VMEM],
        out_specs=HBM,
        scratch_shapes=[
            pltpu.VMEM((4, ROWS, H * DK), BF16),
            pltpu.VMEM((CHUNKS, MESSAGE, DK), BF16),
            pltpu.VMEM((H, DK), BF16),
            pltpu.VMEM((2, DK), jnp.int32),
            pltpu.SemaphoreType.DMA((6,)),
            pltpu.SemaphoreType.DMA((4,)),
        ],
        **params(0, 4 * MIB, 60 * MIB),
        name="pack",
    )(q, k, v, dy, gates, named, logits)


def kind_rows(first, second, first_weight, second_weight):
    row = lax.broadcasted_iota(jnp.int32, (8, DK), 0)
    kind = row.astype(F32)
    shared = (row == MEMS).astype(F32)
    hit_first = jnp.where(row < MEMS, (kind == first).astype(F32), 0.0)
    hit_second = jnp.where(row < MEMS, (kind == second).astype(F32), 0.0)
    return hit_first + hit_second + shared, hit_first * first_weight + hit_second * second_weight + shared


def running_sums(gate):
    t = lax.broadcasted_iota(jnp.int32, (DK, DK), 0)
    s = lax.broadcasted_iota(jnp.int32, (DK, DK), 1)
    gate = gate.astype(BF16)
    return mm(gate, (t <= s).astype(BF16)), mm(gate, jnp.ones((DK, DK), BF16))


def token_rows(buf):
    mask_rows, weight_rows, gate_rows = [], [], []
    for j in range(CHUNKS):
        small = buf[j, 4 * ROWS : MESSAGE, :].astype(F32)
        mask, weight = kind_rows(small[8:9], small[9:10], small[10:11], small[11:12])
        mask_rows.append(mask)
        weight_rows.append(weight)
        gate_rows.append(mask * small[0:1])
    mask, weight, gate = (jnp.concatenate(r, 0) for r in (mask_rows, weight_rows, gate_rows))
    return (mask, weight) + running_sums(gate)


def piled(total):
    parts = [total[8 * j : 8 * j + 8] for j in range(CHUNKS)]
    before, after, whole = [], [], []
    for first in range(0, CHUNKS, GROUP):
        group = parts[first : first + GROUP]
        ahead, behind = [jnp.zeros((8, DK), F32)], [group[-1]]
        for j in range(GROUP - 1):
            ahead.append(ahead[-1] + group[j])
            behind.append(behind[-1] + group[GROUP - 2 - j])
        before += ahead
        after += behind[::-1]
        whole.append(behind[-1])
    return jnp.concatenate(before, 0), jnp.concatenate(after, 0), whole


def by_kind(rows, block):
    return (block.reshape(KINDS, DK, DK) * rows[0:KINDS].reshape(KINDS, 1, DK)).reshape(DEEP, DK)


def row_block(rows, r):
    few = jnp.broadcast_to(rows[r : r + 1], (16, DK)).astype(BF16)
    return jnp.concatenate([few] * (DK // 16), 0)


def col_block(cols, r):
    return jnp.broadcast_to(cols[:, r : r + 1], (DK, DK)).astype(BF16)


def tokens(buf, j):
    return (buf[j, n * ROWS : (n + 1) * ROWS, :] for n in range(4))


def states_kernel(scale, buf, local, *refs):
    mine = lax.axis_index("seqi")
    outs, wide = refs[:OTHERS], refs[OTHERS]
    mask, weight, running, total = token_rows(buf)
    before, after, whole = piled(total)
    write_rows = mask * jnp.exp(after - running)
    read_rows = weight * scale * jnp.exp(before + running)
    decay = [jnp.exp(w) for w in whole]
    both = []
    for side, (left, right, rows) in enumerate(((1, 2, write_rows), (0, 3, read_rows))):
        sums = jnp.zeros((DEEP, DK), F32)
        for g in range(GROUPS) if side == 0 else range(GROUPS - 1, -1, -1):
            local[side, g] = sums.astype(BF16)
            group = range(g * GROUP, (g + 1) * GROUP)
            for j in group:
                flipped = buf[j, left * ROWS : (left + 1) * ROWS, :].T
                for e in range(KINDS):
                    wide[side, e * DK : (e + 1) * DK, j * DK : (j + 1) * DK] = flipped * row_block(rows, j * 8 + e)
            facing = jnp.concatenate([buf[j, right * ROWS : (right + 1) * ROWS, :] for j in group], 0)
            grown = mm(wide[side, :, g * GROUP * DK : (g + 1) * GROUP * DK], facing)
            sums = by_kind(decay[g], sums) + grown
        both.append(sums.astype(BF16))
    zone = sum(whole[1:], whole[0])
    coarse = zone.astype(BF16).astype(F32)
    length = jnp.concatenate([coarse, zone - coarse], 0).astype(BF16)
    for hop, out in enumerate(outs):
        z, c = mine // 2, mine % 2
        later = z + hop < GZ if hop > 0 else c == 0
        out[DEEP:STATE, :] = length

        @pl.when(later)
        def _():
            out[0:DEEP, :] = both[0]

        @pl.when(jnp.logical_not(later))
        def _():
            out[0:DEEP, :] = both[1]


def states(scale, messages):
    return pl.pallas_call(
        lambda *refs: states_kernel(scale, *refs),
        out_shape=[shape((2, GROUPS, DEEP, DK), BF16)] + [shape((STATE, DK), BF16)] * OTHERS,
        in_specs=[VMEM],
        out_specs=[VMEM] * (1 + OTHERS),
        scratch_shapes=[pltpu.VMEM((2, DEEP, CHUNKS * DK), BF16)],
        **params(700_000_000, 4 * MIB),
        name="states",
    )(messages)


def split(rows):
    coarse = rows.astype(BF16).astype(F32)
    return coarse, rows - coarse


def cross_kernel(scale, groups, buf, res):
    mask, weight, running, total = token_rows(buf)
    write_row = mask * jnp.exp(total - running)
    read_row = weight * scale * jnp.exp(running)
    part = lambda a, j: a[8 * j : 8 * j + 8]
    barred = jnp.where(mask > 0, running, BIG)
    named = weight > 0
    shifted_col = (running + jnp.where(named, jnp.log(jnp.where(named, weight, 1.0) * scale), -BIG)).T
    t = lax.broadcasted_iota(jnp.int32, (DK, DK), 0)
    lower = t >= lax.broadcasted_iota(jnp.int32, (DK, DK), 1)
    def own_decay(j):
        decay = jnp.zeros((DK, DK), F32)
        for r in range(j * 8, j * 8 + KINDS):
            decay = decay + jnp.exp(shifted_col[:, r : r + 1] - barred[r : r + 1])
        return jnp.where(lower, decay, 0.0)

    def factors(early, late):
        reads, writes, gap = [], [], jnp.zeros((8, DK), F32)
        for i in late:
            coarse, fine = split(part(read_row, i) * jnp.exp(gap))
            reads.append(jnp.concatenate([coarse, fine, coarse, jnp.zeros((8, DK), F32)], 0))
            gap = gap + part(total, i)
        gap = jnp.zeros((8, DK), F32)
        for j in early[::-1]:
            coarse, fine = split(part(write_row, j) * jnp.exp(gap))
            writes.insert(0, jnp.concatenate([coarse, coarse, fine, jnp.zeros((8, DK), F32)], 0))
            gap = gap + part(total, j)
        reads, writes = (jnp.concatenate(r, 1).astype(BF16) for r in (reads, writes))
        return mm(reads, writes, TN)

    def tile(add, early, late, decay):
        stack = lambda n, js: jnp.concatenate([buf[j, n * ROWS : (n + 1) * ROWS, :] for j in js], 0)
        q, dy = stack(0, late), stack(3, late)
        k, v = stack(1, early), stack(2, early)
        attend = (mm(q, k, NT) * decay).astype(BF16)
        grads = (mm(dy, v, NT) * decay).astype(BF16)
        for n, js, left, right, dims in (
            (0, late, attend, v, NN),
            (1, late, grads, k, NN),
            (2, early, grads, q, TN),
            (3, early, attend, dy, TN),
        ):
            value = mm(left, right, dims)
            for place, j in enumerate(js):
                add(j, n, value[place * ROWS : (place + 1) * ROWS])

    for g in groups:
        first = g * GROUP
        sums = {}

        def add(j, n, value):
            sums[j, n] = sums[j, n] + value if (j, n) in sums else value

        for pair in ((first, first + 1), (first + 2, first + 3)):
            ends = [own_decay(j) for j in pair]
            below = factors(pair[:1], pair[1:])
            empty = jnp.zeros((DK, DK), F32)
            decay = jnp.concatenate(
                [jnp.concatenate([ends[0], empty], 1), jnp.concatenate([below, ends[1]], 1)], 0
            )
            tile(add, pair, pair, decay)
        early, late = (first, first + 1), (first + 2, first + 3)
        tile(add, early, late, factors(early, late))
        for (j, n), value in sums.items():
            res[j - groups[0] * GROUP, n] = value


def cross(scale, groups, messages):
    return pl.pallas_call(
        lambda *refs: cross_kernel(scale, groups, *refs),
        out_shape=shape((len(groups) * GROUP, 4, ROWS, DK), F32),
        in_specs=[VMEM],
        out_specs=VMEM,
        **params(400_000_000 * len(groups), 2 * MIB * len(groups)),
        name="cross",
    )(messages)


def entering(mine, zone, arrived, lengths):
    z, c = mine // 2, mine % 2
    lengths[mine] = zone
    sources = [lax.rem(z + GZ - hop, GZ) * 2 + c for hop in range(1, GZ)]
    sources += [lax.rem(z + GZ - hop, GZ) * 2 + 1 - c for hop in range(GZ)]
    for source, ref in zip(sources, arrived):
        tail = ref[DEEP:STATE, :].astype(F32)
        lengths[source] = tail[0:8] + tail[8:16]
    start = [jnp.zeros((DEEP, DK), F32), jnp.zeros((DEEP, DK), F32)]
    for source, ref in zip(sources, arrived):
        low, high = jnp.minimum(source, mine), jnp.maximum(source, mine)
        gap = jnp.zeros((8, DK), F32)
        for other in range(ZONES):
            inside = jnp.logical_and(low < other, other < high).astype(F32)
            gap = gap + inside * lengths[other]
        earlier = (source < mine).astype(F32)
        factor = jnp.exp(gap)
        block = ref[0:DEEP, :].astype(F32)
        start[0] = start[0] + by_kind(factor * earlier, block)
        start[1] = start[1] + by_kind(factor * (1.0 - earlier), block)
    return start


def turned(state):
    return jnp.concatenate([state[e * DK : (e + 1) * DK].T for e in range(KINDS)], 0)


def finish_kernel(scale, buf, part, rest, local, *refs):
    arrived, (out, lengths) = refs[: ZONES - 1], refs[ZONES - 1 :]
    mask, weight, running, total = token_rows(buf)
    before, after, whole = piled(total)
    read_col = (weight * scale * jnp.exp(before + running)).T
    write_col = (mask * jnp.exp(after - running)).T
    start = entering(lax.axis_index("seqi"), sum(whole[1:], whole[0]), arrived, lengths)
    for g in range(GROUPS):
        group = range(g * GROUP, (g + 1) * GROUP)
        ahead = sum(whole[:g], jnp.zeros((8, DK), F32))
        behind = sum(whole[g + 1 :], jnp.zeros((8, DK), F32))
        state = [
            (local[side, g].astype(F32) + by_kind(jnp.exp(gap), start[side])).astype(BF16)
            for side, gap in enumerate((ahead, behind))
        ]
        flipped = [turned(block) for block in state]
        blocks = [list(tokens(buf, j)) for j in group]
        for cols, jobs in (
            (read_col, ((0, state[0]), (3, flipped[0]))),
            (write_col, ((1, state[1]), (2, flipped[1]))),
        ):
            spread = [[col_block(cols, j * 8 + e) for e in range(KINDS)] for j in group]
            for source, right in jobs:
                n = (0, 3, 2, 1)[source]
                sums = jnp.concatenate([part[j, n] if j < SOONER else rest[j - SOONER, n] for j in group], 0)
                for e in range(KINDS):
                    left = jnp.concatenate([blocks[i][source] * spread[i][e] for i in range(GROUP)], 0)
                    sums = sums + mm(left, right[e * DK : (e + 1) * DK])
                for i, j in enumerate(group):
                    out[j, n * ROWS : (n + 1) * ROWS, :] = sums[i * ROWS : (i + 1) * ROWS].astype(BF16)


def finish(scale, messages, part, rest, local, arrived):
    return pl.pallas_call(
        lambda *refs: finish_kernel(scale, *refs),
        out_shape=shape((CHUNKS, 4 * ROWS, DK), BF16),
        in_specs=[VMEM] * (3 + ZONES),
        out_specs=VMEM,
        scratch_shapes=[pltpu.VMEM((ZONES, 8, DK), F32)],
        **params(1_300_000_000, 8 * MIB),
        name="finish",
    )(messages, part, rest, local, *arrived)


def unpack_kernel(arrived, *refs):
    outs, stage, sems = refs[:4], refs[4], refs[5]
    stores = []
    for n, out in enumerate(outs):
        rows = slice(n * ROWS, (n + 1) * ROWS)
        for h in range(H):
            stage[n, :, h * DK : (h + 1) * DK] = arrived[h, rows, :]
        store = pltpu.make_async_copy(stage.at[n], out.at[0], sems.at[n])
        store.start()
        stores.append(store)
    for store in stores:
        store.wait()


def unpack(arrived):
    return pl.pallas_call(
        unpack_kernel,
        out_shape=[shape((1, ROWS, H * DK), BF16)] * 4,
        in_specs=[VMEM],
        out_specs=[HBM] * 4,
        scratch_shapes=[pltpu.VMEM((4, ROWS, H * DK), BF16), pltpu.SemaphoreType.DMA((4,))],
        **params(0, 4 * MIB),
        name="unpack",
    )(arrived)


def body(queries, keys, values, log_decay, routes, route_logits, cotangent):
    scale = 2.0 / math.sqrt(DK * ROWS * GX * GY * ZONES)
    packed = pack(queries, keys, values, cotangent, log_decay[:, 0, :], routes[0].T, route_logits[0].T)
    messages = lax.all_to_all(packed, ("seqo", "mem"), 0, 0, tiled=True)
    local, to_sibling, *sent = states(scale, messages)
    sibling = [(i, i ^ 1) for i in range(ZONES)]
    arrived = [
        lax.ppermute(block, "seqi", [(i, (i + 2 * hop) % ZONES) for i in range(ZONES)])
        for hop, block in enumerate(sent, 1)
    ]
    beside = [lax.ppermute(to_sibling, "seqi", sibling)]
    part = cross(scale, tuple(range(GROUPS - 1)), messages)
    arrived, part, messages = lax.optimization_barrier((arrived, part, messages))
    beside += [lax.ppermute(block, "seqi", sibling) for block in arrived]
    rest = cross(scale, (GROUPS - 1,), messages)
    results = finish(scale, messages, part, rest, local, arrived + beside)
    returned = lax.all_to_all(results, ("seqo", "mem"), 0, 0, tiled=True)
    return tuple(unpack(returned))


def solution(mesh):
    tokens_spec = P(("seqi", "seqo"), "mem", None)
    return jax.shard_map(
        body,
        mesh=mesh,
        in_specs=(tokens_spec,) * 3 + (P(None, ("seqi", "seqo"), "mem"),) + (tokens_spec,) * 3,
        out_specs=(tokens_spec,) * 4,
        check_vma=False,
    )
```

```python
import math

import jax
import jax.numpy as jnp
from jax import lax
from jax.experimental import pallas as pl
from jax.experimental.pallas import tpu as pltpu
from jax.sharding import PartitionSpec as P

H = 16
DK = 128
ROWS = 128
MEMS = 4
KINDS = MEMS + 1
GX = 4
GY = 4
GZ = 4
CHUNKS = GX * GY
GROUP = 4
GROUPS = CHUNKS // GROUP
MESSAGE = 4 * ROWS + 16
DEEP = KINDS * DK
STATE = DEEP + 16
ZONES = 2 * GZ
OTHERS = GZ
BIG = 1e30
F32 = jnp.float32
BF16 = jnp.bfloat16
MIB = 1 << 20

NT = (((1,), (1,)), ((), ()))
TN = (((0,), (0,)), ((), ()))
NN = (((1,), (0,)), ((), ()))


def mm(a, b, dims=NN):
    return lax.dot_general(a, b, dims, preferred_element_type=F32)


VMEM = pl.BlockSpec(memory_space=pltpu.VMEM)
HBM = pl.BlockSpec(memory_space=pltpu.HBM)


def params(flops, moved, grant=20 * MIB):
    return dict(
        compiler_params=pltpu.CompilerParams(vmem_limit_bytes=grant),
        cost_estimate=pl.CostEstimate(flops=flops, bytes_accessed=moved, transcendentals=0),
    )


def shape(dims, dtype):
    return jax.ShapeDtypeStruct(dims, dtype)


def pack_kernel(q, k, v, dy, *refs):
    small, (logits, out, held, stage, gates, named, in_sems, out_sems) = refs[:2], refs[2:]
    fetches = [
        pltpu.make_async_copy(ref, place, in_sems.at[4 + n])
        for n, (ref, place) in enumerate(zip(small, (gates, named)))
    ]
    for fetch in fetches:
        fetch.start()
    loads = [pltpu.make_async_copy(ref.at[0], held.at[n], in_sems.at[n]) for n, ref in enumerate((q, k, v, dy))]
    for load in loads:
        load.start()
    for fetch in fetches:
        fetch.wait()
    row = lax.broadcasted_iota(jnp.int32, (16, DK), 0)
    kinds = named[...].astype(F32)
    scores = logits[...].astype(F32)
    margin = scores[0:1] - scores[1:2]
    meta = jnp.zeros((16, DK), F32)
    for place, value in (
        (8, kinds[0:1]),
        (9, kinds[1:2]),
        (10, jax.nn.sigmoid(margin)),
        (11, jax.nn.sigmoid(-margin)),
    ):
        meta = jnp.where(row == place, value, meta)
    rates = gates[...].astype(F32)
    for h in range(H):
        stage[h, 4 * ROWS : MESSAGE, :] = jnp.where(row == 0, rates[h : h + 1], meta).astype(BF16)
    stores = []
    for n, load in enumerate(loads):
        load.wait()
        for h in range(H):
            stage[h, n * ROWS : (n + 1) * ROWS, :] = held[n, :, h * DK : (h + 1) * DK]
        last = ROWS + 16 if n == 3 else ROWS
        part = pl.ds(n * ROWS, last)
        store = pltpu.make_async_copy(stage.at[:, part, :], out.at[:, part, :], out_sems.at[n])
        store.start()
        stores.append(store)
    for store in stores:
        store.wait()


def pack(q, k, v, dy, gates, named, logits):
    return pl.pallas_call(
        pack_kernel,
        out_shape=shape((CHUNKS, MESSAGE, DK), BF16),
        in_specs=[HBM] * 6 + [VMEM],
        out_specs=HBM,
        scratch_shapes=[
            pltpu.VMEM((4, ROWS, H * DK), BF16),
            pltpu.VMEM((CHUNKS, MESSAGE, DK), BF16),
            pltpu.VMEM((H, DK), BF16),
            pltpu.VMEM((2, DK), jnp.int32),
            pltpu.SemaphoreType.DMA((6,)),
            pltpu.SemaphoreType.DMA((4,)),
        ],
        **params(0, 4 * MIB, 60 * MIB),
        name="pack",
    )(q, k, v, dy, gates, named, logits)


def kind_rows(first, second, first_weight, second_weight):
    row = lax.broadcasted_iota(jnp.int32, (8, DK), 0)
    kind = row.astype(F32)
    shared = (row == MEMS).astype(F32)
    hit_first = jnp.where(row < MEMS, (kind == first).astype(F32), 0.0)
    hit_second = jnp.where(row < MEMS, (kind == second).astype(F32), 0.0)
    return hit_first + hit_second + shared, hit_first * first_weight + hit_second * second_weight + shared


def running_sums(gate):
    t = lax.broadcasted_iota(jnp.int32, (DK, DK), 0)
    s = lax.broadcasted_iota(jnp.int32, (DK, DK), 1)
    gate = gate.astype(BF16)
    return mm(gate, (t <= s).astype(BF16)), mm(gate, jnp.ones((DK, DK), BF16))


def token_rows(buf):
    mask_rows, weight_rows, gate_rows = [], [], []
    for j in range(CHUNKS):
        small = buf[j, 4 * ROWS : MESSAGE, :].astype(F32)
        mask, weight = kind_rows(small[8:9], small[9:10], small[10:11], small[11:12])
        mask_rows.append(mask)
        weight_rows.append(weight)
        gate_rows.append(mask * small[0:1])
    mask, weight, gate = (jnp.concatenate(r, 0) for r in (mask_rows, weight_rows, gate_rows))
    return (mask, weight) + running_sums(gate)


def piled(total):
    parts = [total[8 * j : 8 * j + 8] for j in range(CHUNKS)]
    before, after, whole = [], [], []
    for first in range(0, CHUNKS, GROUP):
        group = parts[first : first + GROUP]
        ahead, behind = [jnp.zeros((8, DK), F32)], [group[-1]]
        for j in range(GROUP - 1):
            ahead.append(ahead[-1] + group[j])
            behind.append(behind[-1] + group[GROUP - 2 - j])
        before += ahead
        after += behind[::-1]
        whole.append(behind[-1])
    return jnp.concatenate(before, 0), jnp.concatenate(after, 0), whole


def by_kind(rows, block):
    return (block.reshape(KINDS, DK, DK) * rows[0:KINDS].reshape(KINDS, 1, DK)).reshape(DEEP, DK)


def row_block(rows, r):
    few = jnp.broadcast_to(rows[r : r + 1], (16, DK)).astype(BF16)
    return jnp.concatenate([few] * (DK // 16), 0)


def col_block(cols, r):
    return jnp.broadcast_to(cols[:, r : r + 1], (DK, DK)).astype(BF16)


def tokens(buf, j):
    return (buf[j, n * ROWS : (n + 1) * ROWS, :] for n in range(4))


def states_kernel(scale, buf, local, *refs):
    mine = lax.axis_index("seqi")
    outs, wide = refs[:OTHERS], refs[OTHERS]
    mask, weight, running, total = token_rows(buf)
    before, after, whole = piled(total)
    write_rows = mask * jnp.exp(after - running)
    read_rows = weight * scale * jnp.exp(before + running)
    decay = [jnp.exp(w) for w in whole]
    both = []
    for side, (left, right, rows) in enumerate(((1, 2, write_rows), (0, 3, read_rows))):
        sums = jnp.zeros((DEEP, DK), F32)
        for g in range(GROUPS) if side == 0 else range(GROUPS - 1, -1, -1):
            local[side, g] = sums.astype(BF16)
            group = range(g * GROUP, (g + 1) * GROUP)
            for j in group:
                flipped = buf[j, left * ROWS : (left + 1) * ROWS, :].T
                for e in range(KINDS):
                    wide[side, e * DK : (e + 1) * DK, j * DK : (j + 1) * DK] = flipped * row_block(rows, j * 8 + e)
            facing = jnp.concatenate([buf[j, right * ROWS : (right + 1) * ROWS, :] for j in group], 0)
            grown = mm(wide[side, :, g * GROUP * DK : (g + 1) * GROUP * DK], facing)
            sums = by_kind(decay[g], sums) + grown
        both.append(sums.astype(BF16))
    zone = sum(whole[1:], whole[0])
    coarse = zone.astype(BF16).astype(F32)
    length = jnp.concatenate([coarse, zone - coarse], 0).astype(BF16)
    for hop, out in enumerate(outs):
        z, c = mine // 2, mine % 2
        later = z + hop < GZ if hop > 0 else c == 0
        out[DEEP:STATE, :] = length

        @pl.when(later)
        def _():
            out[0:DEEP, :] = both[0]

        @pl.when(jnp.logical_not(later))
        def _():
            out[0:DEEP, :] = both[1]


def states(scale, messages):
    return pl.pallas_call(
        lambda *refs: states_kernel(scale, *refs),
        out_shape=[shape((2, GROUPS, DEEP, DK), BF16)] + [shape((STATE, DK), BF16)] * OTHERS,
        in_specs=[VMEM],
        out_specs=[VMEM] * (1 + OTHERS),
        scratch_shapes=[pltpu.VMEM((2, DEEP, CHUNKS * DK), BF16)],
        **params(700_000_000, 4 * MIB),
        name="states",
    )(messages)


def split(rows):
    coarse = rows.astype(BF16).astype(F32)
    return coarse, rows - coarse


def cross_kernel(scale, buf, res):
    mask, weight, running, total = token_rows(buf)
    write_row = mask * jnp.exp(total - running)
    read_row = weight * scale * jnp.exp(running)
    part = lambda a, j: a[8 * j : 8 * j + 8]
    barred = jnp.where(mask > 0, running, BIG)
    named = weight > 0
    shifted_col = (running + jnp.where(named, jnp.log(jnp.where(named, weight, 1.0) * scale), -BIG)).T
    t = lax.broadcasted_iota(jnp.int32, (DK, DK), 0)
    lower = t >= lax.broadcasted_iota(jnp.int32, (DK, DK), 1)
    def own_decay(j):
        decay = jnp.zeros((DK, DK), F32)
        for r in range(j * 8, j * 8 + KINDS):
            decay = decay + jnp.exp(shifted_col[:, r : r + 1] - barred[r : r + 1])
        return jnp.where(lower, decay, 0.0)

    def factors(early, late):
        reads, writes, gap = [], [], jnp.zeros((8, DK), F32)
        for i in late:
            coarse, fine = split(part(read_row, i) * jnp.exp(gap))
            reads.append(jnp.concatenate([coarse, fine, coarse, jnp.zeros((8, DK), F32)], 0))
            gap = gap + part(total, i)
        gap = jnp.zeros((8, DK), F32)
        for j in early[::-1]:
            coarse, fine = split(part(write_row, j) * jnp.exp(gap))
            writes.insert(0, jnp.concatenate([coarse, coarse, fine, jnp.zeros((8, DK), F32)], 0))
            gap = gap + part(total, j)
        reads, writes = (jnp.concatenate(r, 1).astype(BF16) for r in (reads, writes))
        return mm(reads, writes, TN)

    def tile(add, early, late, decay):
        stack = lambda n, js: jnp.concatenate([buf[j, n * ROWS : (n + 1) * ROWS, :] for j in js], 0)
        q, dy = stack(0, late), stack(3, late)
        k, v = stack(1, early), stack(2, early)
        attend = (mm(q, k, NT) * decay).astype(BF16)
        grads = (mm(dy, v, NT) * decay).astype(BF16)
        for n, js, left, right, dims in (
            (0, late, attend, v, NN),
            (1, late, grads, k, NN),
            (2, early, grads, q, TN),
            (3, early, attend, dy, TN),
        ):
            value = mm(left, right, dims)
            for place, j in enumerate(js):
                add(j, n, value[place * ROWS : (place + 1) * ROWS])

    for g in range(GROUPS):
        first = g * GROUP
        sums = {}

        def add(j, n, value):
            sums[j, n] = sums[j, n] + value if (j, n) in sums else value

        for pair in ((first, first + 1), (first + 2, first + 3)):
            ends = [own_decay(j) for j in pair]
            below = factors(pair[:1], pair[1:])
            empty = jnp.zeros((DK, DK), F32)
            decay = jnp.concatenate(
                [jnp.concatenate([ends[0], empty], 1), jnp.concatenate([below, ends[1]], 1)], 0
            )
            tile(add, pair, pair, decay)
        early, late = (first, first + 1), (first + 2, first + 3)
        tile(add, early, late, factors(early, late))
        for (j, n), value in sums.items():
            res[j, n] = value


def cross(scale, messages):
    return pl.pallas_call(
        lambda *refs: cross_kernel(scale, *refs),
        out_shape=shape((CHUNKS, 4, ROWS, DK), F32),
        in_specs=[VMEM],
        out_specs=VMEM,
        **params(2_000_000_000, 6 * MIB),
        name="cross",
    )(messages)


def entering(mine, zone, arrived, lengths):
    z, c = mine // 2, mine % 2
    lengths[mine] = zone
    sources = [lax.rem(z + GZ - hop, GZ) * 2 + c for hop in range(1, GZ)]
    sources += [lax.rem(z + GZ - hop, GZ) * 2 + 1 - c for hop in range(GZ)]
    for source, ref in zip(sources, arrived):
        tail = ref[DEEP:STATE, :].astype(F32)
        lengths[source] = tail[0:8] + tail[8:16]
    start = [jnp.zeros((DEEP, DK), F32), jnp.zeros((DEEP, DK), F32)]
    for source, ref in zip(sources, arrived):
        low, high = jnp.minimum(source, mine), jnp.maximum(source, mine)
        gap = jnp.zeros((8, DK), F32)
        for other in range(ZONES):
            inside = jnp.logical_and(low < other, other < high).astype(F32)
            gap = gap + inside * lengths[other]
        earlier = (source < mine).astype(F32)
        factor = jnp.exp(gap)
        block = ref[0:DEEP, :].astype(F32)
        start[0] = start[0] + by_kind(factor * earlier, block)
        start[1] = start[1] + by_kind(factor * (1.0 - earlier), block)
    return start


def turned(state):
    return jnp.concatenate([state[e * DK : (e + 1) * DK].T for e in range(KINDS)], 0)


def finish_kernel(scale, buf, part, local, *refs):
    arrived, (out, lengths) = refs[: ZONES - 1], refs[ZONES - 1 :]
    mask, weight, running, total = token_rows(buf)
    before, after, whole = piled(total)
    read_col = (weight * scale * jnp.exp(before + running)).T
    write_col = (mask * jnp.exp(after - running)).T
    start = entering(lax.axis_index("seqi"), sum(whole[1:], whole[0]), arrived, lengths)
    for g in range(GROUPS):
        group = range(g * GROUP, (g + 1) * GROUP)
        ahead = sum(whole[:g], jnp.zeros((8, DK), F32))
        behind = sum(whole[g + 1 :], jnp.zeros((8, DK), F32))
        state = [
            (local[side, g].astype(F32) + by_kind(jnp.exp(gap), start[side])).astype(BF16)
            for side, gap in enumerate((ahead, behind))
        ]
        flipped = [turned(block) for block in state]
        blocks = [list(tokens(buf, j)) for j in group]
        for cols, jobs in (
            (read_col, ((0, state[0]), (3, flipped[0]))),
            (write_col, ((1, state[1]), (2, flipped[1]))),
        ):
            spread = [[col_block(cols, j * 8 + e) for e in range(KINDS)] for j in group]
            for source, right in jobs:
                n = (0, 3, 2, 1)[source]
                sums = jnp.concatenate([part[j, n] for j in group], 0)
                for e in range(KINDS):
                    left = jnp.concatenate([blocks[i][source] * spread[i][e] for i in range(GROUP)], 0)
                    sums = sums + mm(left, right[e * DK : (e + 1) * DK])
                for i, j in enumerate(group):
                    out[j, n * ROWS : (n + 1) * ROWS, :] = sums[i * ROWS : (i + 1) * ROWS].astype(BF16)


def finish(scale, messages, part, local, arrived):
    return pl.pallas_call(
        lambda *refs: finish_kernel(scale, *refs),
        out_shape=shape((CHUNKS, 4 * ROWS, DK), BF16),
        in_specs=[VMEM] * (2 + ZONES),
        out_specs=VMEM,
        scratch_shapes=[pltpu.VMEM((ZONES, 8, DK), F32)],
        **params(1_300_000_000, 8 * MIB),
        name="finish",
    )(messages, part, local, *arrived)


def unpack_kernel(arrived, *refs):
    outs, stage, sems = refs[:4], refs[4], refs[5]
    stores = []
    for n, out in enumerate(outs):
        rows = slice(n * ROWS, (n + 1) * ROWS)
        for h in range(H):
            stage[n, :, h * DK : (h + 1) * DK] = arrived[h, rows, :]
        store = pltpu.make_async_copy(stage.at[n], out.at[0], sems.at[n])
        store.start()
        stores.append(store)
    for store in stores:
        store.wait()


def unpack(arrived):
    return pl.pallas_call(
        unpack_kernel,
        out_shape=[shape((1, ROWS, H * DK), BF16)] * 4,
        in_specs=[VMEM],
        out_specs=[HBM] * 4,
        scratch_shapes=[pltpu.VMEM((4, ROWS, H * DK), BF16), pltpu.SemaphoreType.DMA((4,))],
        **params(0, 4 * MIB),
        name="unpack",
    )(arrived)


def body(queries, keys, values, log_decay, routes, route_logits, cotangent):
    scale = 2.0 / math.sqrt(DK * ROWS * GX * GY * ZONES)
    packed = pack(queries, keys, values, cotangent, log_decay[:, 0, :], routes[0].T, route_logits[0].T)
    messages = lax.all_to_all(packed, ("seqo", "mem"), 0, 0, tiled=True)
    local, to_sibling, *sent = states(scale, messages)
    sibling = [(i, i ^ 1) for i in range(ZONES)]
    ring = lambda hop: [(i, (i + 2 * hop) % ZONES) for i in range(ZONES)]
    farthest = lax.ppermute(sent[1], "seqi", ring(2))
    arrived = [lax.ppermute(sent[0], "seqi", ring(1)), farthest, lax.ppermute(sent[2], "seqi", ring(3))]
    beside = [lax.ppermute(to_sibling, "seqi", sibling)]
    part = cross(scale, messages)
    arrived, part = lax.optimization_barrier((arrived, part))
    beside += [lax.ppermute(block, "seqi", sibling) for block in arrived]
    results = finish(scale, messages, part, local, arrived + beside)
    returned = lax.all_to_all(results, ("seqo", "mem"), 0, 0, tiled=True)
    return tuple(unpack(returned))


def solution(mesh):
    tokens_spec = P(("seqi", "seqo"), "mem", None)
    return jax.shard_map(
        body,
        mesh=mesh,
        in_specs=(tokens_spec,) * 3 + (P(None, ("seqi", "seqo"), "mem"),) + (tokens_spec,) * 3,
        out_specs=(tokens_spec,) * 4,
        check_vma=False,
    )
```
